32 devices in a mesh: groups: 2 (over y), fsdp: 4 (over x, core), tensor: 4 (over z).
Axes of the slice: x: 2, y: 2, z: 4, core: 2. Of those that a mesh axis runs over, the one named last changes fastest.
Arguments:
- tokens: bfloat16 [1024, 8192], P(('groups', 'fsdp'), 'tensor'), parts along dimension 0, may hold values from -6 to 6
- hidden_cotangent: bfloat16 [1024, 14336], P(('groups', 'fsdp'), 'tensor'), parts along dimension 0, may hold values from -6 to 6
- gate_weight: bfloat16 [4096, 14336], P('fsdp', 'tensor'), may hold values from -0.09375 to 0.09375
- up_weight: bfloat16 [4096, 14336], P('fsdp', 'tensor'), may hold values from -0.09375 to 0.09375
- gate_kept: int32 [32, 112], P(None, 'tensor'), may hold values from 0 to 63, as said below
- up_kept: int32 [32, 112], P(None, 'tensor'), may hold values from 0 to 63, as said below
- example_number: int32 [1024], P(('groups', 'fsdp')), parts along dimension 0, may hold values from 0 to 3, as said below
- clip_norm: float32 [1], replicated, may hold values from 1 to 2
Outputs:
- hidden: bfloat16 [1024, 14336], P(('groups', 'fsdp'), 'tensor'), parts along dimension 0
- gate_grad: bfloat16 [8192, 14336], P(('groups', 'fsdp'), 'tensor'), parts along dimension 0
- up_grad: bfloat16 [8192, 14336], P(('groups', 'fsdp'), 'tensor'), parts along dimension 0
- token_grad: bfloat16 [1024, 8192], P(('groups', 'fsdp'), 'tensor'), parts along dimension 0
The draws below stay inside these ranges and needn't reach their ends.
There are 2 independent parts, one for each index of `groups`. The reference program is written for one: setup_inputs(seed, part) draws one part's arguments, and reference() takes and returns one part's arrays. A program takes and returns all parts, laid end to end along the dimension named above; an argument that names none is the same for every part. Nothing has to cross between parts.
Inputs may be any that keep to these rules, and one draw needn't show every extreme that they name: `gate_kept`: each column lists 32 different row blocks. `up_kept`: each column lists 32 different row blocks. `example_number`: on each group of 128 consecutive tokens the numbers never fall and take every value from 0 to 3.
All inputs are finite; a program needn't handle non-finite values.
Results may differ from the reference program's by a relative error of at most 0.0095.
Values may be sent and summed in bfloat16 or wider, within the bound.
No kernel may reach another device: no remote copies, remote signals or barrier semaphores. Data moves between devices by JAX's collectives and lax.ppermute only.
A program may use at most 384 MiB of HBM per device.

```python
import math
import jax
import jax.numpy as jnp
from jax import lax

D = 8192
FFW = 14336
BLK = 128
KEEP = 32
TOK_DEV = 128
EX_DEV = 4
TOKENS = 512
SLOTS = 4096
FFL = 3584
N_FSDP = 4
N_TENSOR = 4


def kept_blocks(key):
    subkeys = jax.random.split(key, FFW // BLK)

    def single(subkey):
        return jax.random.permutation(subkey, D // BLK)[:KEEP]
    chosen = jax.vmap(single)(subkeys)
    return chosen.T.astype(jnp.int32)


def draw_gate_kept(key, part):
    key = jax.random.fold_in(key, 11)
    return kept_blocks(key)


def draw_up_kept(key, part):
    key = jax.random.fold_in(key, 12)
    return kept_blocks(key)


def draw_example_number(key, part):
    key = jax.random.fold_in(key, 13)
    subkeys = jax.random.split(key, TOKENS // TOK_DEV)

    def single(subkey):
        boundary = jax.random.permutation(subkey, TOK_DEV - 1)[:EX_DEV - 1] + 1
        position = jnp.arange(TOK_DEV, dtype=jnp.int32)
        return jnp.sum((boundary[None, :] <= position[:, None]).astype(jnp.int32), axis=1)
    return jax.vmap(single)(subkeys).reshape(TOKENS).astype(jnp.int32)


def draw_tokens(key, part):
    key = jax.random.fold_in(key, 14)
    values = jax.random.truncated_normal(key, -6.0, 6.0, (TOKENS, D), jnp.float32)
    return values.astype(jnp.bfloat16)


def draw_hidden_cotangent(key, part):
    key = jax.random.fold_in(key, 15)
    values = jax.random.truncated_normal(key, -6.0, 6.0, (TOKENS, FFW), jnp.float32)
    return values.astype(jnp.bfloat16)


def block_levels(own_key, dims, cuts, smallest, top_value):
    level = 1.0
    for dim, blocks in cuts:
        draws = jax.random.uniform(jax.random.fold_in(jax.random.fold_in(own_key, 6), dim), (blocks,), jnp.float32, smallest / len(cuts), top_value / len(cuts))
        level = level * jnp.repeat(jnp.exp(draws), dims[dim] // blocks).reshape((-1,) + (1,) * (len(dims) - 1 - dim))
    return level


def bell_draw(stream_key, dims, scale, bound, cuts=(), held_as=jnp.bfloat16):
    factor_of = block_levels(stream_key, dims, cuts, -0.22, 0.18) if cuts else 1.0
    values = jax.random.normal(stream_key, dims, jnp.float32) * scale * factor_of
    return jnp.minimum(jnp.maximum(values, -bound), bound).astype(held_as)


def setup_inputs(seed: int = 0, part: int = 0) -> dict:
    arg_keys = jax.random.split(jax.random.key(seed), 9)
    own_keys = jax.random.split(jax.random.fold_in(arg_keys[8], part), 9)
    return {
        "tokens": draw_tokens(jax.random.fold_in(jax.random.fold_in(arg_keys[8], part), 71), part),
        "hidden_cotangent": draw_hidden_cotangent(jax.random.fold_in(jax.random.fold_in(arg_keys[8], part), 71), part),
        "gate_weight": bell_draw(arg_keys[2], (SLOTS, FFW), SLOTS ** -0.5, 0.09375, ((0, 4), (1, 4))),
        "up_weight": bell_draw(arg_keys[3], (SLOTS, FFW), SLOTS ** -0.5, 0.09375, ((0, 4), (1, 4))),
        "gate_kept": draw_gate_kept(jax.random.fold_in(arg_keys[8], 71), part),
        "up_kept": draw_up_kept(jax.random.fold_in(arg_keys[8], 71), part),
        "example_number": draw_example_number(jax.random.fold_in(jax.random.fold_in(arg_keys[8], part), 71), part),
        "clip_norm": jnp.clip(jax.random.uniform(arg_keys[7], (1,), jnp.float32, 1.0, 2.0), 1.0, 2.0),
    }


def expand_dense(kept, compact):
    row_blocks = D // BLK
    levels = jnp.arange(row_blocks, dtype=jnp.int32)
    placed = (kept[:, :, None] == levels[None, None, :]).astype(jnp.float32)
    per_column = jnp.repeat(placed, BLK, axis=1)
    weights = compact.astype(jnp.float32).reshape(KEEP, BLK, FFW)
    dense = jnp.einsum('kfi,krf->irf', per_column, weights, precision=lax.Precision.HIGHEST)
    return dense.reshape(D, FFW).astype(jnp.bfloat16)

def mask_matrix(kept):
    levels = jnp.arange(D // BLK, dtype=jnp.int32)
    return lax.optimization_barrier(jnp.sum((kept[:, None, :] == levels[None, :, None]).astype(jnp.float32), axis=0))

def pair_term(kept_mask, token_pairs, cotangent):
    shaped = cotangent.astype(jnp.float32).reshape(TOK_DEV, FFW // BLK, BLK)
    own_pairs = jnp.einsum('tjc,sjc->jts', shaped, shaped, precision=lax.Precision.HIGHEST)
    reached = jnp.einsum('ij,its->jts', kept_mask, token_pairs, precision=lax.Precision.HIGHEST)
    return lax.optimization_barrier(jnp.sum(reached * own_pairs, axis=0))

def slot_index(kept):
    offsets = jnp.arange(SLOTS, dtype=jnp.int32) % BLK
    return jnp.repeat(kept, BLK, axis=0) * BLK + offsets[:, None]

def compact_grad(shard_tokens, kept, scaled):
    chosen = jnp.take(shard_tokens, slot_index(kept), axis=1).astype(jnp.float32)
    shaped = scaled.astype(jnp.float32).reshape(TOK_DEV, FFW // BLK, BLK)
    term = jnp.einsum('tgj,tjc->gjc', chosen, shaped, precision=lax.Precision.HIGHEST)
    return term.reshape(SLOTS, FFW)

def reference(tokens, hidden_cotangent, gate_weight, up_weight, gate_kept, up_kept, example_number, clip_norm):
    gate_dense = expand_dense(gate_kept, gate_weight)
    up_dense = expand_dense(up_kept, up_weight)
    gate_sum = jnp.dot(tokens, gate_dense, preferred_element_type=jnp.float32)
    up_sum = jnp.dot(tokens, up_dense, preferred_element_type=jnp.float32)
    sigmoid_gate = jax.nn.sigmoid(gate_sum)
    silu_gate = gate_sum * sigmoid_gate
    hidden = (silu_gate * up_sum).astype(jnp.bfloat16)
    incoming = hidden_cotangent.astype(jnp.float32)
    gate_cot = (incoming * up_sum * sigmoid_gate * (1.0 + gate_sum * (1.0 - sigmoid_gate))).astype(jnp.bfloat16)
    up_cot = (incoming * silu_gate).astype(jnp.bfloat16)
    gate_mask = mask_matrix(gate_kept)
    up_mask = mask_matrix(up_kept)
    row_blocks = D // BLK
    square_list = []
    for shard in range(N_FSDP):
        lower = shard * TOK_DEV
        shard_tokens = tokens[lower:lower + TOK_DEV].astype(jnp.float32).reshape(TOK_DEV, row_blocks, BLK)
        token_pairs = jnp.einsum('tib,sib->its', shard_tokens, shard_tokens, precision=lax.Precision.HIGHEST)
        pair_sum = pair_term(gate_mask, token_pairs, gate_cot[lower:lower + TOK_DEV])
        pair_sum = pair_sum + pair_term(up_mask, token_pairs, up_cot[lower:lower + TOK_DEV])
        numbers = example_number[lower:lower + TOK_DEV]
        member = (numbers[:, None] == jnp.arange(EX_DEV, dtype=jnp.int32)[None, :]).astype(jnp.float32)
        same_example = (numbers[:, None] == numbers[None, :]).astype(jnp.float32)
        square_list.append(jnp.dot(member.T, lax.optimization_barrier(jnp.sum(pair_sum * same_example, axis=1)), precision=lax.Precision.HIGHEST))
    squares = jnp.concatenate(square_list)
    threshold = clip_norm[0] * math.sqrt(D * FFW)
    factor = threshold / jnp.maximum(jnp.sqrt(squares), threshold)
    global_number = jnp.arange(TOKENS, dtype=jnp.int32) // TOK_DEV * EX_DEV + example_number
    token_factor = jnp.take(factor, global_number)
    gate_scaled = (token_factor[:, None] * gate_cot.astype(jnp.float32)).astype(jnp.bfloat16)
    up_scaled = (token_factor[:, None] * up_cot.astype(jnp.float32)).astype(jnp.bfloat16)
    gate_total = jnp.zeros((SLOTS, FFW), jnp.float32)
    up_total = jnp.zeros((SLOTS, FFW), jnp.float32)
    for shard in range(N_FSDP):
        lower = shard * TOK_DEV
        shard_tokens = tokens[lower:lower + TOK_DEV]
        gate_term = compact_grad(shard_tokens, gate_kept, gate_scaled[lower:lower + TOK_DEV]).astype(jnp.bfloat16)
        up_term = compact_grad(shard_tokens, up_kept, up_scaled[lower:lower + TOK_DEV]).astype(jnp.bfloat16)
        gate_term = lax.optimization_barrier(gate_term)
        up_term = lax.optimization_barrier(up_term)
        gate_total = gate_total + gate_term.astype(jnp.float32)
        up_total = up_total + up_term.astype(jnp.float32)
    token_total = jnp.zeros((TOKENS, D), jnp.float32)
    for group in range(N_TENSOR):
        lower = group * FFL
        term = jnp.dot(gate_cot[:, lower:lower + FFL], gate_dense[:, lower:lower + FFL].T, preferred_element_type=jnp.float32)
        term = term + jnp.dot(up_cot[:, lower:lower + FFL], up_dense[:, lower:lower + FFL].T, preferred_element_type=jnp.float32)
        rounded = lax.optimization_barrier(term.astype(jnp.bfloat16))
        token_total = token_total + rounded.astype(jnp.float32)
    return (hidden, gate_total.astype(jnp.bfloat16), up_total.astype(jnp.bfloat16), token_total.astype(jnp.bfloat16))
```

```python
import functools
import math

import jax
import jax.numpy as jnp
from jax import lax
from jax.experimental import pallas as pl
from jax.experimental.pallas import tpu as pltpu
from jax.sharding import PartitionSpec as P

D = 8192
FFW = 14336
BLK = 128
LANES = 128
CORES = 2
CHUNKS = 2
VMEM = 56 * 1024 * 1024
BF16 = jnp.bfloat16
F32 = jnp.float32


def column_group(blocks):
    return max(n for n in (1, 2, 3, 4) if blocks % n == 0)


def params():
    return pltpu.CompilerParams(vmem_limit_bytes=VMEM, dimension_semantics=("arbitrary",))


def block_at(index):
    return pl.ds(pl.multiple_of(index * BLK, BLK), BLK)


def copies_of(pieces, refs, target, sems):
    out = []
    for (array, parts, column), ref in zip(pieces, refs, strict=True):
        for source_row, rows, target_row in parts:
            out.append(
                pltpu.make_async_copy(
                    ref.at[pl.ds(source_row, rows), :],
                    target.at[pl.ds(target_row, rows), pl.ds(column, array.shape[1])],
                    sems.at[len(out)],
                )
            )
    return out


def copy_count(pieces):
    return sum(len(parts) for _, parts, _ in pieces)


def load_pieces(pieces, refs, target, sems):
    @pl.when(pl.program_id(0) == 0)
    def _():
        copies = copies_of(pieces, refs, target, sems)
        for copy in copies:
            copy.start()
        for copy in copies:
            copy.wait()


def forward(pieces, rows, width, gate_own, up_own, gate_weight, up_weight):
    slots, blocks = gate_own.shape
    group = column_group(blocks)
    half = rows // CORES
    depth = slots * BLK
    count = len(pieces)

    def kernel(gk, uk, *refs):
        token_refs = refs[:count]
        wg, wu, keep, send, held, sems = refs[count:]
        load_pieces(pieces, token_refs, held, sems)
        step = pl.program_id(0)
        for j in range(group):
            cols = slice(j * BLK, (j + 1) * BLK)
            for proj, (kept, weight) in enumerate(((gk, wg), (uk, wu))):
                feats = [held[:, block_at(kept[k * blocks + step * group + j])] for k in range(slots)]
                total = jnp.dot(
                    jnp.concatenate(feats, axis=1), weight[:, cols], preferred_element_type=F32
                )
                keep[proj, :, cols] = total[:half].astype(BF16)
                send[proj, :, cols] = total[half:].astype(BF16)

    weight_spec = pl.BlockSpec((depth, group * BLK), lambda i, *_: (0, i))
    out_spec = pl.BlockSpec((2, half, group * BLK), lambda i, *_: (0, 0, i))
    out = jax.ShapeDtypeStruct((2, half, blocks * BLK), BF16)
    return pl.pallas_call(
        kernel,
        out_shape=(out, out),
        grid_spec=pltpu.PrefetchScalarGridSpec(
            num_scalar_prefetch=2,
            grid=(blocks // group,),
            in_specs=[pl.BlockSpec(memory_space=pl.ANY)] * count + [weight_spec] * 2,
            out_specs=(out_spec, out_spec),
            scratch_shapes=[
                pltpu.VMEM((rows, width), BF16),
                pltpu.SemaphoreType.DMA((copy_count(pieces),)),
            ],
        ),
        compiler_params=params(),
        cost_estimate=pl.CostEstimate(
            flops=8 * rows * depth * blocks * BLK,
            bytes_accessed=4 * depth * blocks * BLK + 2 * rows * width,
            transcendentals=0,
        ),
        name="forward",
    )(
        gate_own.reshape(-1),
        up_own.reshape(-1),
        *[piece[0] for piece in pieces],
        gate_weight,
        up_weight,
    )


def transposed(pieces, rows, width):
    step_cols = 1024
    count = len(pieces)

    def kernel(*refs):
        token_refs = refs[:count]
        out, held, sems = refs[count:]
        load_pieces(pieces, token_refs, held, sems)
        step = pl.program_id(0)
        for j in range(step_cols // BLK):
            out[j * BLK : (j + 1) * BLK, :] = held[:, block_at(step * (step_cols // BLK) + j)].T

    return pl.pallas_call(
        kernel,
        out_shape=jax.ShapeDtypeStruct((width, rows), BF16),
        grid=(width // step_cols,),
        in_specs=[pl.BlockSpec(memory_space=pl.ANY)] * count,
        out_specs=pl.BlockSpec((step_cols, rows), lambda i: (i, 0)),
        scratch_shapes=[
            pltpu.VMEM((rows, width), BF16),
            pltpu.SemaphoreType.DMA((copy_count(pieces),)),
        ],
        compiler_params=params(),
        cost_estimate=pl.CostEstimate(
            flops=0, bytes_accessed=12 * rows * width, transcendentals=0
        ),
        name="transposed",
    )(*[piece[0] for piece in pieces])


def reached_pairs(pieces, rows, width, gate_kept, up_kept, same_example):
    keep, blocks = gate_kept.shape
    row_blocks = width // BLK
    count = len(pieces)

    def kernel(gk, uk, *refs):
        token_refs = refs[:count]
        same, out, held, pairs, sems = refs[count:]
        load_pieces(pieces, token_refs, held, sems)
        step = pl.program_id(0)

        @pl.when(step == 0)
        def _():
            def one(i, carry):
                feats = held[:, block_at(i)]
                pairs[i] = lax.dot_general(
                    feats, feats, (((1,), (1,)), ((), ())), preferred_element_type=F32
                )
                return carry

            lax.fori_loop(0, row_blocks, one, 0)

        for proj, kept in enumerate((gk, uk)):
            total = pairs[kept[step]]
            for k in range(1, keep):
                total = total + pairs[kept[k * blocks + step]]
            out[proj, 0] = total * same[...]

    return pl.pallas_call(
        kernel,
        out_shape=jax.ShapeDtypeStruct((2, blocks, rows, rows), F32),
        grid_spec=pltpu.PrefetchScalarGridSpec(
            num_scalar_prefetch=2,
            grid=(blocks,),
            in_specs=[pl.BlockSpec(memory_space=pl.ANY)] * count
            + [pl.BlockSpec((rows, rows), lambda i, *_: (0, 0))],
            out_specs=pl.BlockSpec((2, 1, rows, rows), lambda i, *_: (0, i, 0, 0)),
            scratch_shapes=[
                pltpu.VMEM((rows, width), BF16),
                pltpu.VMEM((row_blocks, rows, rows), F32),
                pltpu.SemaphoreType.DMA((copy_count(pieces),)),
            ],
        ),
        compiler_params=params(),
        cost_estimate=pl.CostEstimate(
            flops=2 * keep * blocks * rows * rows,
            bytes_accessed=40 * blocks * rows * rows,
            transcendentals=0,
        ),
        name="reached_pairs",
    )(gate_kept.reshape(-1), up_kept.reshape(-1), *[piece[0] for piece in pieces], same_example)


def example_squares(reached, cots, member):
    blocks, rows = reached.shape[1:3]
    group = column_group(blocks)
    count = len(cots)

    def kernel(*refs):
        cot_refs = refs[:count]
        reach, members, out, total = refs[count:]
        step = pl.program_id(0)

        @pl.when(step == 0)
        def _():
            total[...] = jnp.zeros_like(total)

        added = total[...]
        for j in range(group):
            cols = slice(j * BLK, (j + 1) * BLK)
            for proj in range(2):
                shaped = jnp.concatenate([ref[proj, :, cols] for ref in cot_refs], axis=0)
                own = lax.dot_general(
                    shaped, shaped, (((1,), (1,)), ((), ())), preferred_element_type=F32
                )
                added = added + own * reach[proj, j]
        total[...] = added

        @pl.when(step == pl.num_programs(0) - 1)
        def _():
            per_token = jnp.sum(total[...], axis=1, keepdims=True)
            per_example = jnp.sum(per_token * members[...], axis=0, keepdims=True)
            out[...] = jnp.broadcast_to(per_example, out.shape)

    cot_rows = cots[0].shape[1]
    return pl.pallas_call(
        kernel,
        out_shape=jax.ShapeDtypeStruct((8, LANES), F32),
        grid=(blocks // group,),
        in_specs=[pl.BlockSpec((2, cot_rows, group * BLK), lambda i: (0, 0, i))] * count
        + [
            pl.BlockSpec((2, group, rows, rows), lambda i: (0, i, 0, 0)),
            pl.BlockSpec((rows, LANES), lambda i: (0, 0)),
        ],
        out_specs=pl.BlockSpec((8, LANES), lambda i: (0, 0)),
        scratch_shapes=[pltpu.VMEM((rows, rows), F32)],
        compiler_params=params(),
        cost_estimate=pl.CostEstimate(
            flops=8 * blocks * rows * rows * BLK,
            bytes_accessed=8 * blocks * rows * rows,
            transcendentals=0,
        ),
        name="example_squares",
    )(*cots, reached, member)


def token_backward(cots, width, gate_own, up_own, gate_weight, up_weight):
    slots, blocks = gate_own.shape
    group = column_group(blocks)
    depth = slots * BLK
    count = len(cots)
    piece_rows = cots[0].shape[1]
    rows = piece_rows * count
    half = rows // CORES

    def kernel(gk, uk, *refs):
        cot_refs = refs[:count]
        wg, wu, keep, send, total = refs[count:]
        step = pl.program_id(0)

        @pl.when(step == 0)
        def _():
            total[...] = jnp.zeros_like(total)

        for j in range(group):
            cols = slice(j * BLK, (j + 1) * BLK)
            for proj, (kept, weight) in enumerate(((gk, wg), (uk, wu))):
                cot = jnp.concatenate([ref[proj, :, cols] for ref in cot_refs], axis=0)
                back = lax.dot_general(
                    cot, weight[:, cols], (((1,), (1,)), ((), ())), preferred_element_type=F32
                )
                for k in range(slots):
                    place = block_at(kept[k * blocks + step * group + j])
                    total[:, place] = total[:, place] + back[:, k * BLK : (k + 1) * BLK]

        @pl.when(step == pl.num_programs(0) - 1)
        def _():
            keep[...] = total[:half].astype(BF16)
            send[...] = total[half:].astype(BF16)

    weight_spec = pl.BlockSpec((depth, group * BLK), lambda i, *_: (0, i))
    out = jax.ShapeDtypeStruct((half, width), BF16)
    out_spec = pl.BlockSpec((half, width), lambda i, *_: (0, 0))
    return pl.pallas_call(
        kernel,
        out_shape=(out, out),
        grid_spec=pltpu.PrefetchScalarGridSpec(
            num_scalar_prefetch=2,
            grid=(blocks // group,),
            in_specs=[
                pl.BlockSpec((2, piece_rows, group * BLK), lambda i, *_: (0, 0, i))
            ]
            * count
            + [weight_spec] * 2,
            out_specs=(out_spec, out_spec),
            scratch_shapes=[pltpu.VMEM((rows, width), F32)],
        ),
        compiler_params=params(),
        cost_estimate=pl.CostEstimate(
            flops=8 * rows * depth * blocks * BLK,
            bytes_accessed=4 * depth * blocks * BLK + 2 * rows * width,
            transcendentals=0,
        ),
        name="token_backward",
    )(gate_own.reshape(-1), up_own.reshape(-1), *cots, gate_weight, up_weight)


def weight_gradients(turned, cots, factors, gate_own, up_own):
    slots, blocks = gate_own.shape
    group = column_group(blocks)
    depth = slots * BLK
    chunks = len(turned)
    per_chunk = len(cots) // chunks
    piece_rows = cots[0].shape[1]
    rows = piece_rows * per_chunk
    width = turned[0].shape[0]

    def kernel(gk, uk, *refs):
        token_refs = refs[:chunks]
        cot_refs = refs[chunks : chunks + len(cots)]
        factor, gate_out, up_out = refs[chunks + len(cots) :]
        step = pl.program_id(0)
        for j in range(group):
            cols = slice(j * BLK, (j + 1) * BLK)
            for proj, (kept, out) in enumerate(((gk, gate_out), (uk, up_out))):
                total = None
                for chunk in range(chunks):
                    cot = jnp.concatenate(
                        [
                            ref[proj, :, cols]
                            for ref in cot_refs[chunk * per_chunk : (chunk + 1) * per_chunk]
                        ],
                        axis=0,
                    )
                    scaled = (
                        factor[chunk * rows : (chunk + 1) * rows, :] * cot.astype(F32)
                    ).astype(BF16)
                    feats = [
                        token_refs[chunk][block_at(kept[k * blocks + step * group + j]), :]
                        for k in range(slots)
                    ]
                    term = jnp.dot(
                        jnp.concatenate(feats, axis=0), scaled, preferred_element_type=F32
                    )
                    total = term if total is None else total + term
                out[:, cols] = total.astype(BF16)

    out = jax.ShapeDtypeStruct((depth, blocks * BLK), BF16)
    out_spec = pl.BlockSpec((depth, group * BLK), lambda i, *_: (0, i))
    return pl.pallas_call(
        kernel,
        out_shape=(out, out),
        grid_spec=pltpu.PrefetchScalarGridSpec(
            num_scalar_prefetch=2,
            grid=(blocks // group,),
            in_specs=[
                pl.BlockSpec((width, rows), lambda i, *_: (0, 0), pipeline_mode=pl.Buffered(1))
            ]
            * chunks
            + [pl.BlockSpec((2, piece_rows, group * BLK), lambda i, *_: (0, 0, i))] * len(cots)
            + [pl.BlockSpec((rows * chunks, LANES), lambda i, *_: (0, 0))],
            out_specs=(out_spec, out_spec),
        ),
        compiler_params=params(),
        cost_estimate=pl.CostEstimate(
            flops=8 * rows * chunks * depth * blocks * BLK,
            bytes_accessed=4 * depth * blocks * BLK + 2 * rows * chunks * width,
            transcendentals=0,
        ),
        name="weight_gradients",
    )(gate_own.reshape(-1), up_own.reshape(-1), *turned, *cots, factors)


def shards(
    tokens,
    hidden_cotangent,
    gate_weight,
    up_weight,
    gate_kept,
    up_kept,
    example_number,
    clip_norm,
    fsdp,
    tensor,
):
    chips = fsdp // CORES
    own_rows, own_features = tokens.shape
    blocks = gate_kept.shape[1]
    width = own_features * tensor
    blocks_each = own_features // BLK
    chunk_rows = own_rows // CHUNKS
    half = chips * chunk_rows
    rows = CORES * half
    z = lax.axis_index("tensor")
    f = lax.axis_index("fsdp")

    def from_chip(value, back):
        pairs = [
            (i, ((i // CORES + back) % chips) * CORES + i % CORES) for i in range(fsdp)
        ]
        return lax.ppermute(value, "fsdp", pairs)

    def from_core(value):
        return lax.ppermute(value, "fsdp", [(i, i ^ 1) for i in range(fsdp)])

    def from_tensor(value, back):
        return lax.ppermute(value, "tensor", [(i, (i + back) % tensor) for i in range(tensor)])

    def renumber(kept):
        return jnp.mod(z - kept // blocks_each, tensor) * blocks_each + kept % blocks_each

    gate_all, up_all = renumber(gate_kept), renumber(up_kept)
    slots = gate_weight.shape[0] // BLK
    gate_own = lax.dynamic_slice_in_dim(gate_all, f * slots, slots, 0)
    up_own = lax.dynamic_slice_in_dim(up_all, f * slots, slots, 0)

    def gather_tokens(chunk):
        own = tokens[chunk * chunk_rows : (chunk + 1) * chunk_rows]
        held = jnp.concatenate([own] + [from_chip(own, s) for s in range(1, chips)], axis=0)
        near = [held]
        for _ in range(1, tensor):
            held = from_tensor(held, 1)
            near.append(held)
        far = [from_core(part) for part in near]
        pieces = []
        for core, parts in enumerate((near, far)):
            for p, part in enumerate(parts):
                pieces.append((part, [(0, half, core * half)], p * own_features))
        mine = [
            (part, [(0, chunk_rows, chunk * chunk_rows)], p * own_features)
            for p, part in enumerate(near)
        ]
        return pieces, mine

    gathered = [gather_tokens(chunk) for chunk in range(CHUNKS)]

    lanes = jnp.arange(LANES, dtype=jnp.int32)
    member = (example_number[:, None] == lanes[None, :]).astype(F32)
    same_example = (example_number[:, None] == example_number[None, :]).astype(F32)

    hidden_parts, own_cots, all_cots, turned = [], [], [], []
    for chunk in range(CHUNKS):
        pieces, _ = gathered[chunk]
        keep, send = forward(pieces, rows, width, gate_own, up_own, gate_weight, up_weight)
        received = from_core(send)

        def pair(s):
            span = slice(s * chunk_rows, (s + 1) * chunk_rows)
            return keep[:, span].astype(F32) + received[:, span].astype(F32)

        sums = pair(0)
        for s in range(1, chips):
            sums = sums + from_chip(pair(s).astype(BF16), -s).astype(F32)
        gate_sum, up_sum = sums[0], sums[1]
        sigmoid_gate = jax.nn.sigmoid(gate_sum)
        silu_gate = gate_sum * sigmoid_gate
        hidden_parts.append((silu_gate * up_sum).astype(BF16))
        incoming = hidden_cotangent[chunk * chunk_rows : (chunk + 1) * chunk_rows].astype(F32)
        gate_cot = incoming * up_sum * sigmoid_gate * (1.0 + gate_sum * (1.0 - sigmoid_gate))
        up_cot = incoming * silu_gate
        cots = jnp.stack([gate_cot.astype(BF16), up_cot.astype(BF16)])
        own_cots.append(cots)
        near = [cots] + [from_chip(cots, s) for s in range(1, chips)]
        all_cots.append(near + [from_core(part) for part in near])

    mine = [piece for _, pieces in gathered for piece in pieces]
    reached = reached_pairs(mine, own_rows, width, gate_all, up_all, same_example)
    turned = [transposed(pieces, rows, width) for pieces, _ in gathered]

    partial = example_squares(reached, own_cots, member)[0]
    squares = partial
    for p in range(1, tensor):
        squares = squares + from_tensor(partial, p)
    threshold = clip_norm[0] * math.sqrt(D * FFW)
    factor = threshold / jnp.maximum(jnp.sqrt(squares), threshold)
    own_factor = jnp.sum(member * factor[None, :], axis=1)
    near = [own_factor] + [from_chip(own_factor, s) for s in range(1, chips)]
    every = near + [from_core(part) for part in near]
    factors = jnp.concatenate(
        [
            part[chunk * chunk_rows : (chunk + 1) * chunk_rows]
            for chunk in range(CHUNKS)
            for part in every
        ]
    )
    factors = jnp.broadcast_to(factors[:, None], (rows * CHUNKS, LANES))

    token_parts = []
    for chunk in range(CHUNKS):
        keep, send = token_backward(
            all_cots[chunk], width, gate_own, up_own, gate_weight, up_weight
        )
        received = from_core(send)

        def share(p):
            span = slice(p * own_features, (p + 1) * own_features)
            return keep[:, span].astype(F32) + received[:, span].astype(F32)

        held = share(tensor - 1)
        for p in range(tensor - 2, -1, -1):
            held = share(p) + from_tensor(held.astype(BF16), -1).astype(F32)
        total = held[:chunk_rows]
        for s in range(1, chips):
            part = held[s * chunk_rows : (s + 1) * chunk_rows].astype(BF16)
            total = total + from_chip(part, -s).astype(F32)
        token_parts.append(total.astype(BF16))

    gate_grad, up_grad = weight_gradients(
        turned, [part for cots in all_cots for part in cots], factors, gate_own, up_own
    )
    hidden = jnp.concatenate(hidden_parts, axis=0)
    token_grad = jnp.concatenate(token_parts, axis=0)
    return (hidden, gate_grad, up_grad, token_grad)


def solution(mesh):
    rows_by_columns = P(("groups", "fsdp"), "tensor")
    return jax.shard_map(
        functools.partial(shards, fsdp=mesh.shape["fsdp"], tensor=mesh.shape["tensor"]),
        mesh=mesh,
        in_specs=(
            rows_by_columns,
            rows_by_columns,
            P("fsdp", "tensor"),
            P("fsdp", "tensor"),
            P(None, "tensor"),
            P(None, "tensor"),
            P(("groups", "fsdp")),
            P(),
        ),
        out_specs=(rows_by_columns,) * 4,
        check_vma=False,
    )
```

```python
import functools
import math

import jax
import jax.numpy as jnp
from jax import lax
from jax.experimental import pallas as pl
from jax.experimental.pallas import tpu as pltpu
from jax.sharding import PartitionSpec as P

D = 8192
FFW = 14336
BLK = 128
LANES = 128
CORES = 2
CHUNKS = 2
VMEM = 56 * 1024 * 1024
BF16 = jnp.bfloat16
F32 = jnp.float32


def column_group(blocks):
    return max(n for n in (1, 2, 3, 4) if blocks % n == 0)


def params():
    return pltpu.CompilerParams(vmem_limit_bytes=VMEM, dimension_semantics=("arbitrary",))


def block_at(index):
    return pl.ds(pl.multiple_of(index * BLK, BLK), BLK)


def copies_of(pieces, refs, target, sems):
    out = []
    for (array, parts, column), ref in zip(pieces, refs, strict=True):
        for source_row, rows, target_row in parts:
            out.append(
                pltpu.make_async_copy(
                    ref.at[pl.ds(source_row, rows), :],
                    target.at[pl.ds(target_row, rows), pl.ds(column, array.shape[1])],
                    sems.at[len(out)],
                )
            )
    return out


def copy_count(pieces):
    return sum(len(parts) for _, parts, _ in pieces)


def load_pieces(pieces, refs, target, sems):
    @pl.when(pl.program_id(0) == 0)
    def _():
        copies = copies_of(pieces, refs, target, sems)
        for copy in copies:
            copy.start()
        for copy in copies:
            copy.wait()


def waits(deps):
    return [pl.BlockSpec(memory_space=pl.ANY)] * len(deps)


def forward(pieces, rows, width, gate_own, up_own, gate_weight, up_weight, deps):
    slots, blocks = gate_own.shape
    group = column_group(blocks)
    half = rows // CORES
    depth = slots * BLK
    count = len(pieces)

    def kernel(gk, uk, *refs):
        token_refs = refs[:count]
        wg, wu = refs[count : count + 2]
        keep, send, held, sems = refs[count + 2 + len(deps) :]
        load_pieces(pieces, token_refs, held, sems)
        step = pl.program_id(0)
        for j in range(group):
            cols = slice(j * BLK, (j + 1) * BLK)
            for proj, (kept, weight) in enumerate(((gk, wg), (uk, wu))):
                feats = [held[:, block_at(kept[k * blocks + step * group + j])] for k in range(slots)]
                total = jnp.dot(
                    jnp.concatenate(feats, axis=1), weight[:, cols], preferred_element_type=F32
                )
                keep[proj, :, cols] = total[:half].astype(BF16)
                send[proj, :, cols] = total[half:].astype(BF16)

    weight_spec = pl.BlockSpec((depth, group * BLK), lambda i, *_: (0, i))
    out_spec = pl.BlockSpec((2, half, group * BLK), lambda i, *_: (0, 0, i))
    out = jax.ShapeDtypeStruct((2, half, blocks * BLK), BF16)
    return pl.pallas_call(
        kernel,
        out_shape=(out, out),
        grid_spec=pltpu.PrefetchScalarGridSpec(
            num_scalar_prefetch=2,
            grid=(blocks // group,),
            in_specs=[pl.BlockSpec(memory_space=pl.ANY)] * count + [weight_spec] * 2 + waits(deps),
            out_specs=(out_spec, out_spec),
            scratch_shapes=[
                pltpu.VMEM((rows, width), BF16),
                pltpu.SemaphoreType.DMA((copy_count(pieces),)),
            ],
        ),
        compiler_params=params(),
        cost_estimate=pl.CostEstimate(
            flops=8 * rows * depth * blocks * BLK,
            bytes_accessed=4 * depth * blocks * BLK + 2 * rows * width,
            transcendentals=0,
        ),
        name="forward",
    )(
        gate_own.reshape(-1),
        up_own.reshape(-1),
        *[piece[0] for piece in pieces],
        gate_weight,
        up_weight,
        *deps,
    )


def after(arrays, deps):
    arrays = list(arrays)

    def kernel(*refs):
        pass

    return pl.pallas_call(
        kernel,
        out_shape=[jax.ShapeDtypeStruct(array.shape, array.dtype) for array in arrays],
        in_specs=waits(arrays) + waits(deps),
        out_specs=waits(arrays),
        input_output_aliases={n: n for n in range(len(arrays))},
        cost_estimate=pl.CostEstimate(flops=0, bytes_accessed=0, transcendentals=0),
        name="after",
    )(*arrays, *deps)


def rows_of(array, spans, deps):
    width = array.shape[1]

    def kernel(*refs):
        for (first, count), out in zip(spans, refs[1 + len(deps) :], strict=True):
            out[...] = refs[0][first : first + count, :]

    return pl.pallas_call(
        kernel,
        out_shape=[jax.ShapeDtypeStruct((count, width), array.dtype) for _, count in spans],
        in_specs=[pl.BlockSpec(memory_space=pltpu.VMEM)] + waits(deps),
        out_specs=[pl.BlockSpec(memory_space=pltpu.VMEM)] * len(spans),
        compiler_params=pltpu.CompilerParams(vmem_limit_bytes=VMEM),
        cost_estimate=pl.CostEstimate(
            flops=0, bytes_accessed=4 * array.shape[0] * width, transcendentals=0
        ),
        name="rows_of",
    )(array, *deps)


def turned_weight(weight, deps):
    depth, width = weight.shape
    group = column_group(width // BLK)

    def kernel(source, *refs):
        out = refs[len(deps)]
        for j in range(group):
            cols = slice(j * BLK, (j + 1) * BLK)
            out[cols, :] = source[:, cols].T

    return pl.pallas_call(
        kernel,
        out_shape=jax.ShapeDtypeStruct((width, depth), BF16),
        grid=(width // BLK // group,),
        in_specs=[pl.BlockSpec((depth, group * BLK), lambda i: (0, i))] + waits(deps),
        out_specs=pl.BlockSpec((group * BLK, depth), lambda i: (i, 0)),
        compiler_params=params(),
        cost_estimate=pl.CostEstimate(
            flops=0, bytes_accessed=4 * depth * width, transcendentals=0
        ),
        name="turned_weight",
    )(weight, *deps)


def transposed(pieces, rows, width, deps):
    step_cols = 1024
    count = len(pieces)

    def kernel(*refs):
        token_refs = refs[:count]
        out, held, sems = refs[count + len(deps) :]
        load_pieces(pieces, token_refs, held, sems)
        step = pl.program_id(0)
        for j in range(step_cols // BLK):
            out[j * BLK : (j + 1) * BLK, :] = held[:, block_at(step * (step_cols // BLK) + j)].T

    return pl.pallas_call(
        kernel,
        out_shape=jax.ShapeDtypeStruct((width, rows), BF16),
        grid=(width // step_cols,),
        in_specs=[pl.BlockSpec(memory_space=pl.ANY)] * count + waits(deps),
        out_specs=pl.BlockSpec((step_cols, rows), lambda i: (i, 0)),
        scratch_shapes=[
            pltpu.VMEM((rows, width), BF16),
            pltpu.SemaphoreType.DMA((copy_count(pieces),)),
        ],
        compiler_params=params(),
        cost_estimate=pl.CostEstimate(
            flops=0, bytes_accessed=4 * rows * width, transcendentals=0
        ),
        name="transposed",
    )(*[piece[0] for piece in pieces], *deps)


def chip_share(keep, received, s, chunk_rows, deps):
    width = keep.shape[2]

    def kernel(a, b, *refs):
        refs[len(deps)][...] = (a[...].astype(F32) + b[...].astype(F32)).astype(BF16)

    spec = pl.BlockSpec((1, chunk_rows, width), lambda i: (i, s, 0))
    return pl.pallas_call(
        kernel,
        out_shape=jax.ShapeDtypeStruct((2, chunk_rows, width), BF16),
        grid=(2,),
        in_specs=[spec, spec] + waits(deps),
        out_specs=pl.BlockSpec((1, chunk_rows, width), lambda i: (i, 0, 0)),
        compiler_params=params(),
        cost_estimate=pl.CostEstimate(
            flops=2 * chunk_rows * width, bytes_accessed=12 * chunk_rows * width, transcendentals=0
        ),
        name="chip_share",
    )(keep, received, *deps)


def cotangents(keep, received, arrived, incoming, chunk, chunk_rows, before, deps):
    width = keep.shape[2]
    cols = max(n for n in range(1, 8) if width // BLK % n == 0) * BLK
    unread = list(before) + list(deps)

    def kernel(a, b, *refs):
        others = refs[: len(arrived)]
        cot_in = refs[len(arrived)]
        hidden, cots = refs[len(arrived) + 1 + len(unread) :]
        sums = []
        for proj in range(2):
            total = a[proj].astype(F32) + b[proj].astype(F32)
            for other in others:
                total = total + other[proj].astype(F32)
            sums.append(total)
        gate_sum, up_sum = sums
        sigmoid_gate = jax.nn.sigmoid(gate_sum)
        silu_gate = gate_sum * sigmoid_gate
        hidden[...] = (silu_gate * up_sum).astype(BF16)
        value = cot_in[...].astype(F32)
        slope = sigmoid_gate * (1.0 + gate_sum * (1.0 - sigmoid_gate))
        cots[0] = (value * up_sum * slope).astype(BF16)
        cots[1] = (value * silu_gate).astype(BF16)

    both = pl.BlockSpec((2, chunk_rows, cols), lambda i: (0, 0, i))
    return pl.pallas_call(
        kernel,
        out_shape=(
            jax.ShapeDtypeStruct(incoming.shape, BF16),
            jax.ShapeDtypeStruct((2, chunk_rows, width), BF16),
        ),
        grid=(width // cols,),
        in_specs=[both] * (2 + len(arrived))
        + [pl.BlockSpec((chunk_rows, cols), lambda i: (chunk, i))]
        + waits(unread),
        out_specs=(pl.BlockSpec((chunk_rows, cols), lambda i: (chunk, i)), both),
        input_output_aliases={3 + len(arrived) + n: n for n in range(len(before))},
        compiler_params=params(),
        cost_estimate=pl.CostEstimate(
            flops=20 * chunk_rows * width,
            bytes_accessed=20 * chunk_rows * width,
            transcendentals=chunk_rows * width,
        ),
        name="cotangents",
    )(keep, received, *arrived, incoming, *unread)


def reached_pairs(pieces, rows, width, gate_kept, up_kept, same_example, deps):
    keep, blocks = gate_kept.shape
    row_blocks = width // BLK
    count = len(pieces)

    def kernel(gk, uk, *refs):
        token_refs = refs[:count]
        same = refs[count]
        out, held, pairs, sems = refs[count + 1 + len(deps) :]
        load_pieces(pieces, token_refs, held, sems)
        step = pl.program_id(0)

        @pl.when(step == 0)
        def _():
            def some(i, carry):
                for n in range(8):
                    feats = held[:, block_at(i * 8 + n)]
                    pairs[i * 8 + n] = lax.dot_general(
                        feats, feats, (((1,), (1,)), ((), ())), preferred_element_type=F32
                    )
                return carry

            lax.fori_loop(0, row_blocks // 8, some, 0)

        for proj, kept in enumerate((gk, uk)):
            total = pairs[kept[step]]
            for k in range(1, keep):
                total = total + pairs[kept[k * blocks + step]]
            out[proj, 0] = total * same[...]

    return pl.pallas_call(
        kernel,
        out_shape=jax.ShapeDtypeStruct((2, blocks, rows, rows), F32),
        grid_spec=pltpu.PrefetchScalarGridSpec(
            num_scalar_prefetch=2,
            grid=(blocks,),
            in_specs=[pl.BlockSpec(memory_space=pl.ANY)] * count
            + [pl.BlockSpec((rows, rows), lambda i, *_: (0, 0))]
            + waits(deps),
            out_specs=pl.BlockSpec((2, 1, rows, rows), lambda i, *_: (0, i, 0, 0)),
            scratch_shapes=[
                pltpu.VMEM((rows, width), BF16),
                pltpu.VMEM((row_blocks, rows, rows), F32),
                pltpu.SemaphoreType.DMA((copy_count(pieces),)),
            ],
        ),
        compiler_params=params(),
        cost_estimate=pl.CostEstimate(
            flops=2 * keep * blocks * rows * rows,
            bytes_accessed=40 * blocks * rows * rows,
            transcendentals=0,
        ),
        name="reached_pairs",
    )(
        gate_kept.reshape(-1),
        up_kept.reshape(-1),
        *[piece[0] for piece in pieces],
        same_example,
        *deps,
    )


def example_squares(reached, cots, member, deps):
    blocks, rows = reached.shape[1:3]
    group = column_group(blocks)
    count = len(cots)

    def kernel(*refs):
        cot_refs = refs[:count]
        reach, members = refs[count : count + 2]
        out, total = refs[count + 2 + len(deps) :]
        step = pl.program_id(0)

        @pl.when(step == 0)
        def _():
            total[...] = jnp.zeros_like(total)

        added = total[...]
        for j in range(group):
            cols = slice(j * BLK, (j + 1) * BLK)
            for proj in range(2):
                shaped = jnp.concatenate([ref[proj, :, cols] for ref in cot_refs], axis=0)
                own = lax.dot_general(
                    shaped, shaped, (((1,), (1,)), ((), ())), preferred_element_type=F32
                )
                added = added + own * reach[proj, j]
        total[...] = added

        @pl.when(step == pl.num_programs(0) - 1)
        def _():
            per_token = jnp.sum(total[...], axis=1, keepdims=True)
            per_example = jnp.sum(per_token * members[...], axis=0, keepdims=True)
            out[...] = jnp.broadcast_to(per_example, out.shape)

    cot_rows = cots[0].shape[1]
    return pl.pallas_call(
        kernel,
        out_shape=jax.ShapeDtypeStruct((8, LANES), F32),
        grid=(blocks // group,),
        in_specs=[pl.BlockSpec((2, cot_rows, group * BLK), lambda i: (0, 0, i))] * count
        + [
            pl.BlockSpec((2, group, rows, rows), lambda i: (0, i, 0, 0)),
            pl.BlockSpec((rows, LANES), lambda i: (0, 0)),
        ]
        + waits(deps),
        out_specs=pl.BlockSpec((8, LANES), lambda i: (0, 0)),
        scratch_shapes=[pltpu.VMEM((rows, rows), F32)],
        compiler_params=params(),
        cost_estimate=pl.CostEstimate(
            flops=8 * blocks * rows * rows * BLK,
            bytes_accessed=8 * blocks * rows * rows,
            transcendentals=0,
        ),
        name="example_squares",
    )(*cots, reached, member, *deps)


def token_backward(cots, width, gate_own, up_own, gate_turned, up_turned, deps):
    slots, blocks = gate_own.shape
    group = column_group(blocks)
    depth = slots * BLK
    count = len(cots)
    piece_rows = cots[0].shape[1]
    rows = piece_rows * count
    half = rows // CORES

    def kernel(gk, uk, *refs):
        cot_refs = refs[:count]
        wg, wu = refs[count : count + 2]
        keep, send, total = refs[count + 2 + len(deps) :]
        step = pl.program_id(0)

        @pl.when(step == 0)
        def _():
            total[...] = jnp.zeros_like(total)

        for j in range(group):
            cols = slice(j * BLK, (j + 1) * BLK)
            for proj, (kept, weight) in enumerate(((gk, wg), (uk, wu))):
                cot = jnp.concatenate([ref[proj, :, cols] for ref in cot_refs], axis=0)
                back = jnp.dot(cot, weight[cols, :], preferred_element_type=F32)
                for k in range(slots):
                    place = kept[k * blocks + step * group + j]
                    total[place] = total[place] + back[:, k * BLK : (k + 1) * BLK]

        @pl.when(step == pl.num_programs(0) - 1)
        def _():
            for i in range(width // BLK):
                cols = slice(i * BLK, (i + 1) * BLK)
                keep[:, cols] = total[i, :half].astype(BF16)
                send[:, cols] = total[i, half:].astype(BF16)

    weight_spec = pl.BlockSpec((group * BLK, depth), lambda i, *_: (i, 0))
    out = jax.ShapeDtypeStruct((half, width), BF16)
    out_spec = pl.BlockSpec((half, width), lambda i, *_: (0, 0))
    return pl.pallas_call(
        kernel,
        out_shape=(out, out),
        grid_spec=pltpu.PrefetchScalarGridSpec(
            num_scalar_prefetch=2,
            grid=(blocks // group,),
            in_specs=[
                pl.BlockSpec((2, piece_rows, group * BLK), lambda i, *_: (0, 0, i))
            ]
            * count
            + [weight_spec] * 2
            + waits(deps),
            out_specs=(out_spec, out_spec),
            scratch_shapes=[pltpu.VMEM((width // BLK, rows, BLK), F32)],
        ),
        compiler_params=params(),
        cost_estimate=pl.CostEstimate(
            flops=8 * rows * depth * blocks * BLK,
            bytes_accessed=4 * depth * blocks * BLK + 2 * rows * width,
            transcendentals=0,
        ),
        name="token_backward",
    )(gate_own.reshape(-1), up_own.reshape(-1), *cots, gate_turned, up_turned, *deps)


def added_cuts(arrays, outputs, deps):
    count = len(arrays)

    def kernel(*refs):
        for cuts, out in zip(outputs, refs[count + len(deps) :], strict=True):
            target = 0
            for which, row, rows, col, cols in cuts:
                at = (slice(row, row + rows), slice(col, col + cols))
                total = refs[which[0]][at].astype(F32)
                for n in which[1:]:
                    total = total + refs[n][at].astype(F32)
                out[target : target + rows, :] = total.astype(BF16)
                target += rows

    size = sum(array.shape[0] * array.shape[1] for array in arrays)
    return pl.pallas_call(
        kernel,
        out_shape=[
            jax.ShapeDtypeStruct((sum(cut[2] for cut in cuts), cuts[0][4]), BF16)
            for cuts in outputs
        ],
        in_specs=[pl.BlockSpec(memory_space=pltpu.VMEM)] * count + waits(deps),
        out_specs=[pl.BlockSpec(memory_space=pltpu.VMEM)] * len(outputs),
        compiler_params=pltpu.CompilerParams(vmem_limit_bytes=VMEM),
        cost_estimate=pl.CostEstimate(flops=size, bytes_accessed=4 * size, transcendentals=0),
        name="added_cuts",
    )(*arrays, *deps)


def weight_gradients(turned, cots, factors, gate_own, up_own, deps):
    slots, blocks = gate_own.shape
    group = column_group(blocks)
    depth = slots * BLK
    chunks = len(turned)
    per_chunk = len(cots) // chunks
    piece_rows = cots[0].shape[1]
    rows = piece_rows * per_chunk
    width = turned[0].shape[0]
    steps = blocks // group

    def kernel(gk, uk, *refs):
        token_refs = refs[:chunks]
        cot_refs = refs[chunks : chunks + len(cots)]
        factor = refs[chunks + len(cots)]
        gate_out, up_out = refs[chunks + len(cots) + 1 + len(deps) :]
        step = pl.program_id(0)
        for j in range(group):
            cols = slice(j * BLK, (j + 1) * BLK)
            for proj, (kept, out) in enumerate(((gk, gate_out), (uk, up_out))):
                total = None
                for chunk in range(chunks):
                    cot = jnp.concatenate(
                        [
                            ref[proj, :, cols]
                            for ref in cot_refs[chunk * per_chunk : (chunk + 1) * per_chunk]
                        ],
                        axis=0,
                    )
                    scaled = (
                        factor[chunk * rows : (chunk + 1) * rows, :] * cot.astype(F32)
                    ).astype(BF16)
                    feats = [
                        token_refs[chunk][block_at(kept[k * blocks + step * group + j]), :]
                        for k in range(slots)
                    ]
                    term = jnp.dot(
                        jnp.concatenate(feats, axis=0), scaled, preferred_element_type=F32
                    )
                    total = term if total is None else total + term
                out[:, cols] = total.astype(BF16)

    out = jax.ShapeDtypeStruct((depth, blocks * BLK), BF16)
    out_spec = pl.BlockSpec((depth, group * BLK), lambda i, *_: (0, i))
    operands = [gate_own.reshape(-1), up_own.reshape(-1), *turned, *cots, factors]
    return pl.pallas_call(
        kernel,
        out_shape=(out, out),
        grid_spec=pltpu.PrefetchScalarGridSpec(
            num_scalar_prefetch=2,
            grid=(steps,),
            in_specs=[
                pl.BlockSpec((width, rows), lambda i, *_: (0, 0), pipeline_mode=pl.Buffered(1))
            ]
            * chunks
            + [pl.BlockSpec((2, piece_rows, group * BLK), lambda i, *_: (0, 0, i))]
            * len(cots)
            + [pl.BlockSpec((rows * chunks, LANES), lambda i, *_: (0, 0))]
            + waits(deps),
            out_specs=(out_spec, out_spec),
        ),
        compiler_params=params(),
        cost_estimate=pl.CostEstimate(
            flops=8 * rows * chunks * depth * steps * group * BLK,
            bytes_accessed=4 * depth * steps * group * BLK + 2 * rows * chunks * width,
            transcendentals=0,
        ),
        name="weight_gradients",
    )(*operands, *deps)


def shards(
    tokens,
    hidden_cotangent,
    gate_weight,
    up_weight,
    gate_kept,
    up_kept,
    example_number,
    clip_norm,
    fsdp,
    tensor,
):
    chips = fsdp // CORES
    own_rows, own_features = tokens.shape
    blocks = gate_kept.shape[1]
    width = own_features * tensor
    blocks_each = own_features // BLK
    chunk_rows = own_rows // CHUNKS
    first_rows = chunk_rows // 2
    half = chips * chunk_rows
    rows = CORES * half
    z = lax.axis_index("tensor")
    f = lax.axis_index("fsdp")

    def from_chip(value, back):
        pairs = [
            (i, ((i // CORES + back) % chips) * CORES + i % CORES) for i in range(fsdp)
        ]
        return lax.ppermute(value, "fsdp", pairs)

    def from_core(value):
        return lax.ppermute(value, "fsdp", [(i, i ^ 1) for i in range(fsdp)])

    def from_rank(value, core, back):
        pairs = [
            (i, ((i // CORES + back) % chips) * CORES + (i % CORES + core) % CORES)
            for i in range(fsdp)
        ]
        return lax.ppermute(value, "fsdp", pairs)

    def from_tensor(value, back):
        return lax.ppermute(value, "tensor", [(i, (i + back) % tensor) for i in range(tensor)])

    def renumber(kept):
        return jnp.mod(z - kept // blocks_each, tensor) * blocks_each + kept % blocks_each

    gate_all, up_all = renumber(gate_kept), renumber(up_kept)
    slots = gate_weight.shape[0] // BLK
    gate_own = lax.dynamic_slice_in_dim(gate_all, f * slots, slots, 0)
    up_own = lax.dynamic_slice_in_dim(up_all, f * slots, slots, 0)

    lanes = jnp.arange(LANES, dtype=jnp.int32)
    member = (example_number[:, None] == lanes[None, :]).astype(F32)
    same_example = (example_number[:, None] == example_number[None, :]).astype(F32)

    def piece(array, core, s, p):
        target = core * half + s * chunk_rows
        return (array, [(0, array.shape[0], target)], p * own_features)

    part_0, part_1 = rows_of(tokens, [(0, chunk_rows), (chunk_rows, chunk_rows)], ())
    along = [part_0] + [from_tensor(part_0, p) for p in range(1, tensor)]
    stack = jnp.concatenate([part_1] + [from_chip(part_1, s) for s in range(1, chips)], axis=0)
    (stack,) = after([stack], along[1:])
    pieces_0, mine = [], []
    for p in range(tensor):
        mine.append((along[p], [(0, chunk_rows, 0)], p * own_features))
        for s in range(chips):
            array = along[p] if s == 0 else from_chip(along[p], s)
            pieces_0 += [piece(array, 0, s, p), piece(from_core(array), 1, s, p)]
    middle = tensor // 2
    others = [p for p in range(1, tensor) if p != middle]
    first, second = others[: len(others) // 2], others[len(others) // 2 :]
    direct = {0: stack} | {p: from_tensor(stack, p) for p in range(1, tensor)}
    keep_0, send_0 = forward(
        pieces_0, rows, width, gate_own, up_own, gate_weight, up_weight, [stack]
    )
    send_0, *done = after([send_0] + [direct[p] for p in first], ())
    direct.update(zip(first, done, strict=True))
    received_0 = from_core(send_0)
    gate_turned = turned_weight(gate_weight, [send_0])
    received_0, *done = after([received_0] + [direct[p] for p in second], [gate_turned])
    direct.update(zip(second, done, strict=True))
    leaving_0 = [chip_share(keep_0, received_0, s, chunk_rows, ()) for s in range(1, chips)]
    up_turned = turned_weight(up_weight, leaving_0)
    tokens_0 = transposed(pieces_0, rows, width, [up_turned])
    (direct[middle],) = after([direct[middle]], [tokens_0])
    direct = [direct[p] for p in range(tensor)]
    arrived_0 = [from_chip(part, -s - 1) for s, part in enumerate(leaving_0)]
    pieces_1 = []
    for p, array in enumerate(direct):
        mine.append((array, [(0, chunk_rows, chunk_rows)], p * own_features))
        pieces_1 += [piece(array, 0, 0, p), piece(from_core(array), 1, 0, p)]

    hidden_0, cots_0 = cotangents(
        keep_0, received_0, arrived_0, hidden_cotangent, 0, chunk_rows, (), [direct[middle]]
    )
    far_0 = [from_chip(cots_0, s) for s in range(1, chips)]
    keep_1, send_1 = forward(
        pieces_1, rows, width, gate_own, up_own, gate_weight, up_weight, [cots_0]
    )
    *far_0, send_1 = after(far_0 + [send_1], [keep_1])
    received_1 = from_core(send_1)
    tokens_1 = transposed(pieces_1, rows, width, [send_1])
    (received_1,) = after([received_1], [tokens_1])
    leaving_1 = [chip_share(keep_1, received_1, s, chunk_rows, ()) for s in range(1, chips)]
    arrived_1 = [from_chip(part, -s - 1) for s, part in enumerate(leaving_1)]
    every_0 = [cots_0] + far_0 + [from_core(part) for part in [cots_0] + far_0]
    back_0 = token_backward(
        every_0, width, gate_own, up_own, gate_turned, up_turned, leaving_1
    )
    *arrived_1, sent = after(arrived_1 + [back_0[1]], ())
    received = from_core(sent)
    hidden, cots_1 = cotangents(
        keep_1, received_1, arrived_1, hidden_cotangent, 1, chunk_rows, [hidden_0], back_0[:1]
    )
    far_1 = [from_chip(cots_1, s) for s in range(1, chips)]

    def leave(keep, received, count, deps):
        rest = chunk_rows - count
        outputs = [
            [
                ((0, 1), s * chunk_rows, count, p * own_features, own_features)
                for s in range(chips)
            ]
            for p in range(tensor)
        ]
        if rest:
            outputs += [[((0, 1), s * chunk_rows + count, rest, 0, width)] for s in range(chips)]
        outs = added_cuts([keep, received], outputs, deps)
        return outs[:tensor], outs[tensor:]

    def over_tensor_first(stacks):
        return [stacks[0]] + [from_tensor(stacks[p], -p) for p in range(1, tensor)]

    def then_chips(stacks, count, deps):
        every = tuple(range(len(stacks)))
        outputs = [[(every, s * count, count, 0, own_features)] for s in range(chips)]
        outs = added_cuts(stacks, outputs, deps)
        return [outs[0]] + [from_chip(outs[s], -s) for s in range(1, chips)]

    parts_0, _ = leave(back_0[0], received, chunk_rows, [cots_1])
    crossing_0 = over_tensor_first(parts_0)
    reached = reached_pairs(
        mine, own_rows, width, gate_all, up_all, same_example, parts_0[:1]
    )
    partial = example_squares(reached, [cots_0, cots_1], member, ())
    early = [p for p in range(1, tensor) if p != middle]
    ordered = after(far_1 + [crossing_0[p] for p in early], [partial])
    far_1 = list(ordered[: len(far_1)])
    for p, array in zip(early, ordered[len(far_1) :], strict=True):
        crossing_0[p] = array
    every_1 = [cots_1] + far_1 + [from_core(part) for part in [cots_1] + far_1]
    apart = [from_tensor(partial, p) for p in range(1, tensor)]
    back_1 = token_backward(
        every_1, width, gate_own, up_own, gate_turned, up_turned, apart
    )
    crossing_0[middle], sent, *apart = after([crossing_0[middle], back_1[1]] + apart, ())
    squares = partial[0]
    for array in apart:
        squares = squares + array[0]
    threshold = clip_norm[0] * math.sqrt(D * FFW)
    factor = threshold / jnp.maximum(jnp.sqrt(squares), threshold)
    own_factor = jnp.sum(member * factor[None, :], axis=1)
    factors_near = [own_factor] + [
        from_rank(own_factor, core, s) for core in range(CORES) for s in range(chips) if core or s
    ]
    received = from_core(sent)
    final_0 = then_chips(crossing_0, chunk_rows, [sent])
    factors = jnp.concatenate(
        [
            part[chunk * chunk_rows : (chunk + 1) * chunk_rows]
            for chunk in range(CHUNKS)
            for part in factors_near
        ]
    )
    factors = jnp.broadcast_to(factors[:, None], (rows * CHUNKS, LANES))

    parts_1, rest_1 = leave(back_1[0], received, first_rows, [final_0[0], factors])
    crossing_1 = over_tensor_first(parts_1)
    over_chips = [rest_1[0]] + [from_chip(rest_1[s], -s) for s in range(1, chips)]
    rest = chunk_rows - first_rows

    gate_grad, up_grad = weight_gradients(
        [tokens_0, tokens_1], every_0 + every_1, factors, gate_own, up_own, [parts_1[0]]
    )
    every = tuple(range(chips))
    shares = added_cuts(
        over_chips,
        [[(every, 0, rest, p * own_features, own_features)] for p in range(tensor)],
        [gate_grad],
    )
    late = [shares[0]] + [from_tensor(shares[p], -p) for p in range(1, tensor)]
    final_1 = then_chips(crossing_1, first_rows, [gate_grad])
    parts, cuts = [], []
    for arrays, count in ((final_0, chunk_rows), (final_1, first_rows), (late, rest)):
        places = tuple(range(len(parts), len(parts) + len(arrays)))
        parts += arrays
        cuts.append((places, 0, count, 0, own_features))
    (token_grad,) = added_cuts(parts, [cuts], [gate_grad])
    return (hidden, gate_grad, up_grad, token_grad)


def solution(mesh):
    rows_by_columns = P(("groups", "fsdp"), "tensor")
    return jax.shard_map(
        functools.partial(shards, fsdp=mesh.shape["fsdp"], tensor=mesh.shape["tensor"]),
        mesh=mesh,
        in_specs=(
            rows_by_columns,
            rows_by_columns,
            P("fsdp", "tensor"),
            P("fsdp", "tensor"),
            P(None, "tensor"),
            P(None, "tensor"),
            P(("groups", "fsdp")),
            P(),
        ),
        out_specs=(rows_by_columns,) * 4,
        check_vma=False,
    )
```

```python
import functools
import math

import jax
import jax.numpy as jnp
from jax import lax
from jax.experimental import pallas as pl
from jax.experimental.pallas import tpu as pltpu
from jax.sharding import PartitionSpec as P

D = 8192
FFW = 14336
BLK = 128
LANES = 128
CORES = 2
CHUNKS = 2
MIB = 1024 * 1024
BF16 = jnp.bfloat16
F32 = jnp.float32


def column_group(blocks):
    return max(n for n in range(1, 8) if blocks % n == 0)


def params(held):
    return pltpu.CompilerParams(vmem_limit_bytes=held + 6 * MIB)


def block_at(index):
    return pl.ds(pl.multiple_of(index * BLK, BLK), BLK)


def copies_of(pieces, refs, target, sems):
    out = []
    for (array, parts, column), ref in zip(pieces, refs, strict=True):
        for source_row, rows, target_row in parts:
            out.append(
                pltpu.make_async_copy(
                    ref.at[pl.ds(source_row, rows), :],
                    target.at[pl.ds(target_row, rows), pl.ds(column, array.shape[1])],
                    sems.at[len(out)],
                )
            )
    return out


def copy_count(pieces):
    return sum(len(parts) for _, parts, _ in pieces)


def load_pieces(pieces, refs, target, sems):
    @pl.when(pl.program_id(0) == 0)
    def _():
        copies = copies_of(pieces, refs, target, sems)
        for copy in copies:
            copy.start()
        for copy in copies:
            copy.wait()


MARK = jax.ShapeDtypeStruct((8, LANES), F32)


def mark_spec():
    return pl.BlockSpec((8, LANES), lambda *_: (0, 0))


def mark(ref):
    ref[...] = jnp.zeros(ref.shape, ref.dtype)


def waits(deps):
    return [pl.BlockSpec(memory_space=pl.ANY)] * len(deps)


def forward(pieces, rows, width, gate_own, up_own, gate_weight, up_weight, deps):
    slots, blocks = gate_own.shape
    group = column_group(blocks)
    half = rows // CORES
    depth = slots * BLK
    count = len(pieces)

    def kernel(gk, uk, *refs):
        token_refs = refs[:count]
        wg, wu = refs[count : count + 2]
        keep, send, held, sems = refs[count + 2 + len(deps) :]
        load_pieces(pieces, token_refs, held, sems)
        step = pl.program_id(0)
        for j in range(group):
            cols = slice(j * BLK, (j + 1) * BLK)
            for proj, (kept, weight) in enumerate(((gk, wg), (uk, wu))):
                feats = [held[:, block_at(kept[k * blocks + step * group + j])] for k in range(slots)]
                total = jnp.dot(
                    jnp.concatenate(feats, axis=1), weight[:, cols], preferred_element_type=F32
                )
                keep[proj, :, cols] = total[:half].astype(BF16)
                send[proj, :, cols] = total[half:].astype(BF16)

    weight_spec = pl.BlockSpec((depth, group * BLK), lambda i, *_: (0, i))
    out_spec = pl.BlockSpec((2, half, group * BLK), lambda i, *_: (0, 0, i))
    out = jax.ShapeDtypeStruct((2, half, blocks * BLK), BF16)
    return pl.pallas_call(
        kernel,
        out_shape=(out, out),
        grid_spec=pltpu.PrefetchScalarGridSpec(
            num_scalar_prefetch=2,
            grid=(blocks // group,),
            in_specs=[pl.BlockSpec(memory_space=pl.ANY)] * count + [weight_spec] * 2 + waits(deps),
            out_specs=(out_spec, out_spec),
            scratch_shapes=[
                pltpu.VMEM((rows, width), BF16),
                pltpu.SemaphoreType.DMA((copy_count(pieces),)),
            ],
        ),
        compiler_params=params(50 * MIB),
        cost_estimate=pl.CostEstimate(
            flops=8 * rows * depth * blocks * BLK,
            bytes_accessed=4 * depth * blocks * BLK + 2 * rows * width,
            transcendentals=0,
        ),
        name="forward",
    )(
        gate_own.reshape(-1),
        up_own.reshape(-1),
        *[piece[0] for piece in pieces],
        gate_weight,
        up_weight,
        *deps,
    )


def after(arrays, deps, marked=False):
    arrays = list(arrays)

    def kernel(*refs):
        mark(refs[-1])

    return pl.pallas_call(
        kernel,
        out_shape=[jax.ShapeDtypeStruct(array.shape, array.dtype) for array in arrays] + [MARK],
        in_specs=waits(arrays) + waits(deps),
        out_specs=waits(arrays) + [pl.BlockSpec(memory_space=pltpu.VMEM)],
        input_output_aliases={n: n for n in range(len(arrays))},
        cost_estimate=pl.CostEstimate(flops=0, bytes_accessed=0, transcendentals=0),
        name="after",
    )(*arrays, *deps)[: None if marked else len(arrays)]


def rows_of(array, spans, deps):
    width = array.shape[1]

    def kernel(*refs):
        for (first, count), out in zip(spans, refs[1 + len(deps) :], strict=True):
            out[...] = refs[0][first : first + count, :]

    return pl.pallas_call(
        kernel,
        out_shape=[jax.ShapeDtypeStruct((count, width), array.dtype) for _, count in spans],
        in_specs=[pl.BlockSpec(memory_space=pltpu.VMEM)] + waits(deps),
        out_specs=[pl.BlockSpec(memory_space=pltpu.VMEM)] * len(spans),
        compiler_params=params(4 * MIB),
        cost_estimate=pl.CostEstimate(
            flops=0, bytes_accessed=4 * array.shape[0] * width, transcendentals=0
        ),
        name="rows_of",
    )(array, *deps)


def turned_weight(weight, deps):
    depth, width = weight.shape
    group = column_group(width // BLK)

    def kernel(source, *refs):
        out, done = refs[len(deps) :]
        mark(done)
        for j in range(group):
            cols = slice(j * BLK, (j + 1) * BLK)
            out[cols, :] = source[:, cols].T

    return pl.pallas_call(
        kernel,
        out_shape=(jax.ShapeDtypeStruct((width, depth), BF16), MARK),
        grid=(width // BLK // group,),
        in_specs=[pl.BlockSpec((depth, group * BLK), lambda i: (0, i))] + waits(deps),
        out_specs=(pl.BlockSpec((group * BLK, depth), lambda i: (i, 0)), mark_spec()),
        compiler_params=params(50 * MIB),
        cost_estimate=pl.CostEstimate(
            flops=0, bytes_accessed=4 * depth * width, transcendentals=0
        ),
        name="turned_weight",
    )(weight, *deps)


def transposed(pieces, rows, width, deps):
    step_cols = 1024
    count = len(pieces)

    def kernel(*refs):
        token_refs = refs[:count]
        out, done, held, sems = refs[count + len(deps) :]
        mark(done)
        load_pieces(pieces, token_refs, held, sems)
        step = pl.program_id(0)
        for j in range(step_cols // BLK):
            out[j * BLK : (j + 1) * BLK, :] = held[:, block_at(step * (step_cols // BLK) + j)].T

    return pl.pallas_call(
        kernel,
        out_shape=(jax.ShapeDtypeStruct((width, rows), BF16), MARK),
        grid=(width // step_cols,),
        in_specs=[pl.BlockSpec(memory_space=pl.ANY)] * count + waits(deps),
        out_specs=(pl.BlockSpec((step_cols, rows), lambda i: (i, 0)), mark_spec()),
        scratch_shapes=[
            pltpu.VMEM((rows, width), BF16),
            pltpu.SemaphoreType.DMA((copy_count(pieces),)),
        ],
        compiler_params=params(50 * MIB),
        cost_estimate=pl.CostEstimate(
            flops=0, bytes_accessed=4 * rows * width, transcendentals=0
        ),
        name="transposed",
    )(*[piece[0] for piece in pieces], *deps)


def chip_share(keep, received, s, chunk_rows, deps):
    width = keep.shape[2]

    def kernel(a, b, *refs):
        refs[len(deps)][...] = (a[...].astype(F32) + b[...].astype(F32)).astype(BF16)

    spec = pl.BlockSpec((1, chunk_rows, width), lambda i: (i, s, 0))
    return pl.pallas_call(
        kernel,
        out_shape=jax.ShapeDtypeStruct((2, chunk_rows, width), BF16),
        grid=(2,),
        in_specs=[spec, spec] + waits(deps),
        out_specs=pl.BlockSpec((1, chunk_rows, width), lambda i: (i, 0, 0)),
        compiler_params=params(12 * chunk_rows * width),
        cost_estimate=pl.CostEstimate(
            flops=2 * chunk_rows * width, bytes_accessed=12 * chunk_rows * width, transcendentals=0
        ),
        name="chip_share",
    )(keep, received, *deps)


def cotangents(keep, received, arrived, incoming, chunk, chunk_rows, before, deps):
    width = keep.shape[2]
    cols = column_group(width // BLK) * BLK
    unread = list(before) + list(deps)

    def kernel(a, b, *refs):
        others = refs[: len(arrived)]
        cot_in = refs[len(arrived)]
        hidden, cots, done = refs[len(arrived) + 1 + len(unread) :]
        mark(done)
        sums = []
        for proj in range(2):
            total = a[proj].astype(F32) + b[proj].astype(F32)
            for other in others:
                total = total + other[proj].astype(F32)
            sums.append(total)
        gate_sum, up_sum = sums
        sigmoid_gate = jax.nn.sigmoid(gate_sum)
        silu_gate = gate_sum * sigmoid_gate
        hidden[...] = (silu_gate * up_sum).astype(BF16)
        value = cot_in[...].astype(F32)
        slope = sigmoid_gate * (1.0 + gate_sum * (1.0 - sigmoid_gate))
        cots[0] = (value * up_sum * slope).astype(BF16)
        cots[1] = (value * silu_gate).astype(BF16)

    both = pl.BlockSpec((2, chunk_rows, cols), lambda i: (0, 0, i))
    return pl.pallas_call(
        kernel,
        out_shape=(
            jax.ShapeDtypeStruct(incoming.shape, BF16),
            jax.ShapeDtypeStruct((2, chunk_rows, width), BF16),
            MARK,
        ),
        grid=(width // cols,),
        in_specs=[both] * (2 + len(arrived))
        + [pl.BlockSpec((chunk_rows, cols), lambda i: (chunk, i))]
        + waits(unread),
        out_specs=(pl.BlockSpec((chunk_rows, cols), lambda i: (chunk, i)), both, mark_spec()),
        input_output_aliases={3 + len(arrived) + n: n for n in range(len(before))},
        compiler_params=params(24 * (3 + len(arrived)) * chunk_rows * cols),
        cost_estimate=pl.CostEstimate(
            flops=20 * chunk_rows * width,
            bytes_accessed=20 * chunk_rows * width,
            transcendentals=chunk_rows * width,
        ),
        name="cotangents",
    )(keep, received, *arrived, incoming, *unread)


def reached_pairs(pieces, rows, width, gate_kept, up_kept, same_example, deps):
    keep, blocks = gate_kept.shape
    group = column_group(blocks)
    row_blocks = width // BLK
    count = len(pieces)

    def kernel(gk, uk, *refs):
        token_refs = refs[:count]
        same = refs[count]
        out, done, held, pairs, sems = refs[count + 1 + len(deps) :]
        mark(done)
        load_pieces(pieces, token_refs, held, sems)
        step = pl.program_id(0)

        @pl.when(step == 0)
        def _():
            def some(i, carry):
                for n in range(8):
                    feats = held[:, block_at(i * 8 + n)]
                    pairs[i * 8 + n] = lax.dot_general(
                        feats, feats, (((1,), (1,)), ((), ())), preferred_element_type=F32
                    )
                return carry

            lax.fori_loop(0, row_blocks // 8, some, 0)

        for j in range(group):
            for proj, kept in enumerate((gk, uk)):
                column = step * group + j
                total = pairs[kept[column]]
                for k in range(1, keep):
                    total = total + pairs[kept[k * blocks + column]]
                out[proj, j] = total * same[...]

    return pl.pallas_call(
        kernel,
        out_shape=(jax.ShapeDtypeStruct((2, blocks, rows, rows), F32), MARK),
        grid_spec=pltpu.PrefetchScalarGridSpec(
            num_scalar_prefetch=2,
            grid=(blocks // group,),
            in_specs=[pl.BlockSpec(memory_space=pl.ANY)] * count
            + [pl.BlockSpec((rows, rows), lambda i, *_: (0, 0))]
            + waits(deps),
            out_specs=(
                pl.BlockSpec((2, group, rows, rows), lambda i, *_: (0, i, 0, 0)),
                mark_spec(),
            ),
            scratch_shapes=[
                pltpu.VMEM((rows, width), BF16),
                pltpu.VMEM((row_blocks, rows, rows), F32),
                pltpu.SemaphoreType.DMA((copy_count(pieces),)),
            ],
        ),
        compiler_params=params(50 * MIB),
        cost_estimate=pl.CostEstimate(
            flops=2 * keep * blocks * rows * rows,
            bytes_accessed=40 * blocks * rows * rows,
            transcendentals=0,
        ),
        name="reached_pairs",
    )(
        gate_kept.reshape(-1),
        up_kept.reshape(-1),
        *[piece[0] for piece in pieces],
        same_example,
        *deps,
    )


def example_squares(reached, cots, member, deps):
    blocks, rows = reached.shape[1:3]
    group = column_group(blocks)
    count = len(cots)

    def kernel(*refs):
        cot_refs = refs[:count]
        reach, members = refs[count : count + 2]
        out, total = refs[count + 2 + len(deps) :]
        step = pl.program_id(0)

        @pl.when(step == 0)
        def _():
            total[...] = jnp.zeros_like(total)

        added = total[...]
        for j in range(group):
            cols = slice(j * BLK, (j + 1) * BLK)
            for proj in range(2):
                shaped = jnp.concatenate([ref[proj, :, cols] for ref in cot_refs], axis=0)
                own = lax.dot_general(
                    shaped, shaped, (((1,), (1,)), ((), ())), preferred_element_type=F32
                )
                added = added + own * reach[proj, j]
        total[...] = added

        @pl.when(step == pl.num_programs(0) - 1)
        def _():
            per_token = jnp.sum(total[...], axis=1, keepdims=True)
            per_example = jnp.sum(per_token * members[...], axis=0, keepdims=True)
            out[...] = jnp.broadcast_to(per_example, out.shape)

    cot_rows = cots[0].shape[1]
    return pl.pallas_call(
        kernel,
        out_shape=jax.ShapeDtypeStruct((8, LANES), F32),
        grid=(blocks // group,),
        in_specs=[pl.BlockSpec((2, cot_rows, group * BLK), lambda i: (0, 0, i))] * count
        + [
            pl.BlockSpec((2, group, rows, rows), lambda i: (0, i, 0, 0)),
            pl.BlockSpec((rows, LANES), lambda i: (0, 0)),
        ]
        + waits(deps),
        out_specs=pl.BlockSpec((8, LANES), lambda i: (0, 0)),
        scratch_shapes=[pltpu.VMEM((rows, rows), F32)],
        compiler_params=params((16 * group + 8) * rows * rows + 8 * rows * group * BLK),
        cost_estimate=pl.CostEstimate(
            flops=8 * blocks * rows * rows * BLK,
            bytes_accessed=8 * blocks * rows * rows,
            transcendentals=0,
        ),
        name="example_squares",
    )(*cots, reached, member, *deps)


def token_backward(cots, width, gate_own, up_own, gate_turned, up_turned, deps):
    slots, blocks = gate_own.shape
    group = column_group(blocks)
    depth = slots * BLK
    count = len(cots)
    piece_rows = cots[0].shape[1]
    rows = piece_rows * count
    half = rows // CORES

    def kernel(gk, uk, *refs):
        cot_refs = refs[:count]
        wg, wu = refs[count : count + 2]
        keep, send, done, total = refs[count + 2 + len(deps) :]
        mark(done)
        step = pl.program_id(0)

        @pl.when(step == 0)
        def _():
            total[...] = jnp.zeros_like(total)

        for j in range(group):
            cols = slice(j * BLK, (j + 1) * BLK)
            for proj, (kept, weight) in enumerate(((gk, wg), (uk, wu))):
                cot = jnp.concatenate([ref[proj, :, cols] for ref in cot_refs], axis=0)
                back = jnp.dot(cot, weight[cols, :], preferred_element_type=F32)
                for k in range(slots):
                    place = kept[k * blocks + step * group + j]
                    total[place] = total[place] + back[:, k * BLK : (k + 1) * BLK]

        @pl.when(step == pl.num_programs(0) - 1)
        def _():
            for i in range(width // BLK):
                cols = slice(i * BLK, (i + 1) * BLK)
                keep[:, cols] = total[i, :half].astype(BF16)
                send[:, cols] = total[i, half:].astype(BF16)

    weight_spec = pl.BlockSpec((group * BLK, depth), lambda i, *_: (i, 0))
    out = jax.ShapeDtypeStruct((half, width), BF16)
    out_spec = pl.BlockSpec((half, width), lambda i, *_: (0, 0))
    return pl.pallas_call(
        kernel,
        out_shape=(out, out, MARK),
        grid_spec=pltpu.PrefetchScalarGridSpec(
            num_scalar_prefetch=2,
            grid=(blocks // group,),
            in_specs=[
                pl.BlockSpec((2, piece_rows, group * BLK), lambda i, *_: (0, 0, i))
            ]
            * count
            + [weight_spec] * 2
            + waits(deps),
            out_specs=(out_spec, out_spec, mark_spec()),
            scratch_shapes=[pltpu.VMEM((width // BLK, rows, BLK), F32)],
        ),
        compiler_params=params(50 * MIB),
        cost_estimate=pl.CostEstimate(
            flops=8 * rows * depth * blocks * BLK,
            bytes_accessed=4 * depth * blocks * BLK + 2 * rows * width,
            transcendentals=0,
        ),
        name="token_backward",
    )(gate_own.reshape(-1), up_own.reshape(-1), *cots, gate_turned, up_turned, *deps)


def added_cuts(arrays, outputs, deps):
    count = len(arrays)

    def kernel(*refs):
        *outs, done = refs[count + len(deps) :]
        mark(done)
        for cuts, out in zip(outputs, outs, strict=True):
            target = 0
            for which, row, rows, col, cols in cuts:
                at = (slice(row, row + rows), slice(col, col + cols))
                total = refs[which[0]][at].astype(F32)
                for n in which[1:]:
                    total = total + refs[n][at].astype(F32)
                out[target : target + rows, :] = total.astype(BF16)
                target += rows

    size = sum(array.shape[0] * array.shape[1] for array in arrays)
    return pl.pallas_call(
        kernel,
        out_shape=[
            jax.ShapeDtypeStruct((sum(cut[2] for cut in cuts), cuts[0][4]), BF16)
            for cuts in outputs
        ]
        + [MARK],
        in_specs=[pl.BlockSpec(memory_space=pltpu.VMEM)] * count + waits(deps),
        out_specs=[pl.BlockSpec(memory_space=pltpu.VMEM)] * (len(outputs) + 1),
        compiler_params=params(4 * MIB),
        cost_estimate=pl.CostEstimate(flops=size, bytes_accessed=4 * size, transcendentals=0),
        name="added_cuts",
    )(*arrays, *deps)


def weight_gradients(turned, cots, factors, gate_own, up_own, deps):
    slots, blocks = gate_own.shape
    group = column_group(blocks)
    depth = slots * BLK
    chunks = len(turned)
    per_chunk = len(cots) // chunks
    piece_rows = cots[0].shape[1]
    rows = piece_rows * per_chunk
    width = turned[0].shape[0]
    steps = blocks // group

    def kernel(gk, uk, *refs):
        token_refs = refs[:chunks]
        cot_refs = refs[chunks : chunks + len(cots)]
        factor = refs[chunks + len(cots)]
        gate_out, up_out, done = refs[chunks + len(cots) + 1 + len(deps) :]
        mark(done)
        step = pl.program_id(0)
        for j in range(group):
            cols = slice(j * BLK, (j + 1) * BLK)
            for proj, (kept, out) in enumerate(((gk, gate_out), (uk, up_out))):
                total = None
                for chunk in range(chunks):
                    cot = jnp.concatenate(
                        [
                            ref[proj, :, cols]
                            for ref in cot_refs[chunk * per_chunk : (chunk + 1) * per_chunk]
                        ],
                        axis=0,
                    )
                    scaled = (
                        factor[chunk * rows : (chunk + 1) * rows, :] * cot.astype(F32)
                    ).astype(BF16)
                    feats = [
                        token_refs[chunk][block_at(kept[k * blocks + step * group + j]), :]
                        for k in range(slots)
                    ]
                    term = jnp.dot(
                        jnp.concatenate(feats, axis=0), scaled, preferred_element_type=F32
                    )
                    total = term if total is None else total + term
                out[:, cols] = total.astype(BF16)

    out = jax.ShapeDtypeStruct((depth, blocks * BLK), BF16)
    out_spec = pl.BlockSpec((depth, group * BLK), lambda i, *_: (0, i))
    operands = [gate_own.reshape(-1), up_own.reshape(-1), *turned, *cots, factors]
    return pl.pallas_call(
        kernel,
        out_shape=(out, out, MARK),
        grid_spec=pltpu.PrefetchScalarGridSpec(
            num_scalar_prefetch=2,
            grid=(steps,),
            in_specs=[
                pl.BlockSpec((width, rows), lambda i, *_: (0, 0), pipeline_mode=pl.Buffered(1))
            ]
            * chunks
            + [pl.BlockSpec((2, piece_rows, group * BLK), lambda i, *_: (0, 0, i))]
            * len(cots)
            + [pl.BlockSpec((rows * chunks, LANES), lambda i, *_: (0, 0))]
            + waits(deps),
            out_specs=(out_spec, out_spec, mark_spec()),
        ),
        compiler_params=params(55 * MIB),
        cost_estimate=pl.CostEstimate(
            flops=8 * rows * chunks * depth * steps * group * BLK,
            bytes_accessed=4 * depth * steps * group * BLK + 2 * rows * chunks * width,
            transcendentals=0,
        ),
        name="weight_gradients",
    )(*operands, *deps)


def shards(
    tokens,
    hidden_cotangent,
    gate_weight,
    up_weight,
    gate_kept,
    up_kept,
    example_number,
    clip_norm,
    fsdp,
    tensor,
):
    chips = fsdp // CORES
    own_rows, own_features = tokens.shape
    blocks = gate_kept.shape[1]
    width = own_features * tensor
    blocks_each = own_features // BLK
    chunk_rows = own_rows // CHUNKS
    first_rows = chunk_rows // 2
    half = chips * chunk_rows
    rows = CORES * half
    z = lax.axis_index("tensor")
    f = lax.axis_index("fsdp")

    def from_chip(value, back):
        pairs = [
            (i, ((i // CORES + back) % chips) * CORES + i % CORES) for i in range(fsdp)
        ]
        return lax.ppermute(value, "fsdp", pairs)

    def from_core(value):
        return lax.ppermute(value, "fsdp", [(i, i ^ 1) for i in range(fsdp)])

    def from_rank(value, core, back):
        pairs = [
            (i, ((i // CORES + back) % chips) * CORES + (i % CORES + core) % CORES)
            for i in range(fsdp)
        ]
        return lax.ppermute(value, "fsdp", pairs)

    def from_tensor(value, back):
        return lax.ppermute(value, "tensor", [(i, (i + back) % tensor) for i in range(tensor)])

    def renumber(kept):
        return jnp.mod(z - kept // blocks_each, tensor) * blocks_each + kept % blocks_each

    gate_all, up_all = renumber(gate_kept), renumber(up_kept)
    slots = gate_weight.shape[0] // BLK
    gate_own = lax.dynamic_slice_in_dim(gate_all, f * slots, slots, 0)
    up_own = lax.dynamic_slice_in_dim(up_all, f * slots, slots, 0)

    lanes = jnp.arange(LANES, dtype=jnp.int32)
    member = (example_number[:, None] == lanes[None, :]).astype(F32)
    same_example = (example_number[:, None] == example_number[None, :]).astype(F32)

    def piece(array, core, s, p):
        target = core * half + s * chunk_rows
        return (array, [(0, array.shape[0], target)], p * own_features)

    part_0, part_1 = rows_of(tokens, [(0, chunk_rows), (chunk_rows, chunk_rows)], ())
    along = [part_0] + [from_tensor(part_0, p) for p in range(1, tensor)]
    stack = jnp.concatenate([part_1] + [from_chip(part_1, s) for s in range(1, chips)], axis=0)
    moved = {0: [from_chip(part_0, s) for s in range(1, chips)]}
    last = 0
    for p in sorted(range(1, tensor), key=lambda p: min(p, tensor - p)):
        along[p], stack, *moved[last] = after([along[p], stack] + moved[last], ())
        moved[p] = [from_chip(along[p], s) for s in range(1, chips)]
        last = p
    pieces_0, mine = [], []
    for p in range(tensor):
        mine.append((along[p], [(0, chunk_rows, 0)], p * own_features))
        for s, array in enumerate([along[p]] + moved[p]):
            pieces_0 += [piece(array, 0, s, p), piece(from_core(array), 1, s, p)]
    middle = tensor // 2
    ring = [stack]

    def step_on():
        return [from_tensor(ring[-1], 1)] if len(ring) < tensor else []

    def arrive(moving, arrays, deps):
        if moving + arrays:
            moving = after(moving + arrays, deps)
            ring.extend(moving[: len(moving) - len(arrays)])
        return moving[len(moving) - len(arrays) :]

    moving = step_on()
    keep_0, send_0 = forward(
        pieces_0, rows, width, gate_own, up_own, gate_weight, up_weight, [stack]
    )
    (send_0,) = arrive(moving, [send_0], ())
    moving = step_on()
    received_0 = from_core(send_0)
    gate_turned, gate_done = turned_weight(gate_weight, [send_0])
    arrive(moving, [], [gate_done])
    moving = step_on()
    leaving_0 = [
        chip_share(keep_0, received_0, s, chunk_rows, [gate_done]) for s in range(1, chips)
    ]
    up_turned, up_done = turned_weight(up_weight, leaving_0)
    arrive(moving, [], [up_done])
    while len(ring) < tensor:
        ring += step_on()
    tokens_0, tokens_0_done = transposed(pieces_0, rows, width, [up_done, ring[-1]])
    arrived_0 = [from_chip(part, -s - 1) for s, part in enumerate(leaving_0)]
    pieces_1 = []
    for p, array in enumerate(ring):
        mine.append((array, [(0, chunk_rows, chunk_rows)], p * own_features))
        pieces_1 += [piece(array, 0, 0, p), piece(from_core(array), 1, 0, p)]

    hidden_0, cots_0, cots_0_done = cotangents(
        keep_0, received_0, arrived_0, hidden_cotangent, 0, chunk_rows, (), [tokens_0_done]
    )
    far_0 = [from_chip(cots_0, s) for s in range(1, chips)]
    keep_1, send_1 = forward(
        pieces_1, rows, width, gate_own, up_own, gate_weight, up_weight, [cots_0_done]
    )
    *far_0, send_1 = after(far_0 + [send_1], [keep_1])
    received_1 = from_core(send_1)
    tokens_1, tokens_1_done = transposed(pieces_1, rows, width, [send_1])
    leaving_1 = [
        chip_share(keep_1, received_1, s, chunk_rows, [tokens_1_done]) for s in range(1, chips)
    ]
    arrived_1 = [from_chip(part, -s - 1) for s, part in enumerate(leaving_1)]
    every_0 = [cots_0] + far_0 + [from_core(part) for part in [cots_0] + far_0]
    back_0 = token_backward(
        every_0, width, gate_own, up_own, gate_turned, up_turned, leaving_1
    )
    *arrived_1, sent = after(arrived_1 + [back_0[1]], ())
    received = from_core(sent)
    hidden, cots_1, cots_1_done = cotangents(
        keep_1, received_1, arrived_1, hidden_cotangent, 1, chunk_rows, [hidden_0], [back_0[2]]
    )
    far_1 = [from_chip(cots_1, s) for s in range(1, chips)]

    def leave(keep, received, count, deps):
        rest = chunk_rows - count
        outputs = [
            [
                ((0, 1), s * chunk_rows, count, p * own_features, own_features)
                for s in range(chips)
            ]
            for p in range(tensor)
        ]
        if rest:
            outputs += [[((0, 1), s * chunk_rows + count, rest, 0, width)] for s in range(chips)]
        outs = added_cuts([keep, received], outputs, deps)
        return outs[:tensor], outs[tensor:-1], outs[-1]

    def over_tensor_first(stacks):
        return [stacks[0]] + [from_tensor(stacks[p], -p) for p in range(1, tensor)]

    def then_chips(stacks, count, deps):
        every = tuple(range(len(stacks)))
        outputs = [[(every, s * count, count, 0, own_features)] for s in range(chips)]
        outs = added_cuts(stacks, outputs, deps)
        return [outs[0]] + [from_chip(outs[s], -s) for s in range(1, chips)], outs[-1]

    parts_0, _, parts_0_done = leave(back_0[0], received, chunk_rows, [cots_1_done])
    crossing_0 = over_tensor_first(parts_0)
    reached, reached_done = reached_pairs(
        mine, own_rows, width, gate_all, up_all, same_example, [parts_0_done]
    )
    early = [p for p in range(1, tensor) if p != middle]
    *ordered, ordered_done = after(
        far_1 + [crossing_0[p] for p in early], [reached_done], marked=True
    )
    far_1 = list(ordered[: len(far_1)])
    for p, array in zip(early, ordered[len(far_1) :], strict=True):
        crossing_0[p] = array
    every_1 = [cots_1] + far_1 + [from_core(part) for part in [cots_1] + far_1]
    partial = example_squares(reached, [cots_0, cots_1], member, [ordered_done])
    apart = [from_tensor(partial, p) for p in range(1, tensor)]
    back_1 = token_backward(
        every_1, width, gate_own, up_own, gate_turned, up_turned, [partial]
    )
    crossing_0[middle], sent, *apart = after([crossing_0[middle], back_1[1]] + apart, ())
    squares = partial[0]
    for array in apart:
        squares = squares + array[0]
    threshold = clip_norm[0] * math.sqrt(D * FFW)
    factor = threshold / jnp.maximum(jnp.sqrt(squares), threshold)
    own_factor = jnp.sum(member * factor[None, :], axis=1)
    factors_near = [own_factor] + [
        from_rank(own_factor, core, s) for core in range(CORES) for s in range(chips) if core or s
    ]
    received = from_core(sent)
    final_0, final_0_done = then_chips(crossing_0, chunk_rows, [back_1[2]])
    factors = jnp.concatenate(
        [
            part[chunk * chunk_rows : (chunk + 1) * chunk_rows]
            for chunk in range(CHUNKS)
            for part in factors_near
        ]
    )
    factors = jnp.broadcast_to(factors[:, None], (rows * CHUNKS, LANES))

    parts_1, rest_1, parts_1_done = leave(back_1[0], received, first_rows, [final_0_done])
    crossing_1 = over_tensor_first(parts_1)
    over_chips = [rest_1[0]] + [from_chip(rest_1[s], -s) for s in range(1, chips)]
    rest = chunk_rows - first_rows

    gate_grad, up_grad, grads_done = weight_gradients(
        [tokens_0, tokens_1], every_0 + every_1, factors, gate_own, up_own, [parts_1_done]
    )
    every = tuple(range(chips))
    shares = added_cuts(
        over_chips,
        [[(every, 0, rest, p * own_features, own_features)] for p in range(tensor)],
        [grads_done],
    )
    late = [shares[0]] + [from_tensor(shares[p], -p) for p in range(1, tensor)]
    final_1, _ = then_chips(crossing_1, first_rows, [grads_done])
    parts, cuts = [], []
    for arrays, count in ((final_0, chunk_rows), (final_1, first_rows), (late, rest)):
        places = tuple(range(len(parts), len(parts) + len(arrays)))
        parts += arrays
        cuts.append((places, 0, count, 0, own_features))
    token_grad, _ = added_cuts(parts, [cuts], [grads_done])
    return (hidden, gate_grad, up_grad, token_grad)


def solution(mesh):
    rows_by_columns = P(("groups", "fsdp"), "tensor")
    return jax.shard_map(
        functools.partial(shards, fsdp=mesh.shape["fsdp"], tensor=mesh.shape["tensor"]),
        mesh=mesh,
        in_specs=(
            rows_by_columns,
            rows_by_columns,
            P("fsdp", "tensor"),
            P("fsdp", "tensor"),
            P(None, "tensor"),
            P(None, "tensor"),
            P(("groups", "fsdp")),
            P(),
        ),
        out_specs=(rows_by_columns,) * 4,
        check_vma=False,
    )
```

```python
import functools
import math

import jax
import jax.numpy as jnp
from jax import lax
from jax.experimental import pallas as pl
from jax.experimental.pallas import tpu as pltpu
from jax.sharding import PartitionSpec as P

D = 8192
FFW = 14336
BLK = 128
LANES = 128
CORES = 2
CHUNKS = 2
MIB = 1024 * 1024
BF16 = jnp.bfloat16
F32 = jnp.float32


def column_group(blocks):
    return max(n for n in range(1, 8) if blocks % n == 0 and (n == 1 or n < blocks))


def params(held):
    return pltpu.CompilerParams(vmem_limit_bytes=held + 6 * MIB)


def block_at(index):
    return pl.ds(pl.multiple_of(index * BLK, BLK), BLK)


def copies_of(pieces, refs, target, sems):
    out = []
    for (array, parts, column), ref in zip(pieces, refs, strict=True):
        for source_row, rows, target_row in parts:
            out.append(
                pltpu.make_async_copy(
                    ref.at[pl.ds(source_row, rows), :],
                    target.at[pl.ds(target_row, rows), pl.ds(column, array.shape[1])],
                    sems.at[len(out)],
                )
            )
    return out


def copy_count(pieces):
    return sum(len(parts) for _, parts, _ in pieces)


def load_pieces(pieces, refs, target, sems):
    @pl.when(pl.program_id(0) == 0)
    def _():
        copies = copies_of(pieces, refs, target, sems)
        for copy in copies:
            copy.start()
        for copy in copies:
            copy.wait()


MARK = jax.ShapeDtypeStruct((8, LANES), F32)


def mark_spec():
    return pl.BlockSpec((8, LANES), lambda *_: (0, 0))


def mark(ref):
    ref[...] = jnp.zeros(ref.shape, ref.dtype)


def waits(deps):
    return [pl.BlockSpec(memory_space=pl.ANY)] * len(deps)


def forward(pieces, rows, width, gate_own, up_own, gate_weight, up_weight, deps):
    slots, blocks = gate_own.shape
    group = column_group(blocks)
    half = rows // CORES
    depth = slots * BLK
    count = len(pieces)

    def kernel(gk, uk, *refs):
        token_refs = refs[:count]
        wg, wu = refs[count : count + 2]
        keep, send, held, sems = refs[count + 2 + len(deps) :]
        load_pieces(pieces, token_refs, held, sems)
        step = pl.program_id(0)
        for j in range(group):
            cols = slice(j * BLK, (j + 1) * BLK)
            for proj, (kept, weight) in enumerate(((gk, wg), (uk, wu))):
                feats = [held[:, block_at(kept[k * blocks + step * group + j])] for k in range(slots)]
                total = jnp.dot(
                    jnp.concatenate(feats, axis=1), weight[:, cols], preferred_element_type=F32
                )
                keep[proj, :, cols] = total[:half].astype(BF16)
                send[proj, :, cols] = total[half:].astype(BF16)

    weight_spec = pl.BlockSpec((depth, group * BLK), lambda i, *_: (0, i))
    out_spec = pl.BlockSpec((2, half, group * BLK), lambda i, *_: (0, 0, i))
    out = jax.ShapeDtypeStruct((2, half, blocks * BLK), BF16)
    return pl.pallas_call(
        kernel,
        out_shape=(out, out),
        grid_spec=pltpu.PrefetchScalarGridSpec(
            num_scalar_prefetch=2,
            grid=(blocks // group,),
            in_specs=[pl.BlockSpec(memory_space=pl.ANY)] * count + [weight_spec] * 2 + waits(deps),
            out_specs=(out_spec, out_spec),
            scratch_shapes=[
                pltpu.VMEM((rows, width), BF16),
                pltpu.SemaphoreType.DMA((copy_count(pieces),)),
            ],
        ),
        compiler_params=params(50 * MIB),
        cost_estimate=pl.CostEstimate(
            flops=8 * rows * depth * blocks * BLK,
            bytes_accessed=4 * depth * blocks * BLK + 2 * rows * width,
            transcendentals=0,
        ),
        name="forward",
    )(
        gate_own.reshape(-1),
        up_own.reshape(-1),
        *[piece[0] for piece in pieces],
        gate_weight,
        up_weight,
        *deps,
    )


def after(arrays, deps):
    arrays = list(arrays)

    def kernel(*refs):
        mark(refs[-1])

    return pl.pallas_call(
        kernel,
        out_shape=[jax.ShapeDtypeStruct(array.shape, array.dtype) for array in arrays] + [MARK],
        in_specs=waits(arrays) + waits(deps),
        out_specs=waits(arrays) + [pl.BlockSpec(memory_space=pltpu.VMEM)],
        input_output_aliases={n: n for n in range(len(arrays))},
        cost_estimate=pl.CostEstimate(flops=0, bytes_accessed=0, transcendentals=0),
        name="after",
    )(*arrays, *deps)[: len(arrays)]


def rows_of(array, spans, deps):
    width = array.shape[1]

    def kernel(*refs):
        for (first, count), out in zip(spans, refs[1 + len(deps) :], strict=True):
            out[...] = refs[0][first : first + count, :]

    return pl.pallas_call(
        kernel,
        out_shape=[jax.ShapeDtypeStruct((count, width), array.dtype) for _, count in spans],
        in_specs=[pl.BlockSpec(memory_space=pltpu.VMEM)] + waits(deps),
        out_specs=[pl.BlockSpec(memory_space=pltpu.VMEM)] * len(spans),
        compiler_params=params(4 * MIB),
        cost_estimate=pl.CostEstimate(
            flops=0, bytes_accessed=4 * array.shape[0] * width, transcendentals=0
        ),
        name="rows_of",
    )(array, *deps)


def turned_weight(weight, deps):
    depth, width = weight.shape
    group = column_group(width // BLK)

    def kernel(source, *refs):
        out, done = refs[len(deps) :]
        mark(done)
        for j in range(group):
            cols = slice(j * BLK, (j + 1) * BLK)
            out[cols, :] = source[:, cols].T

    return pl.pallas_call(
        kernel,
        out_shape=(jax.ShapeDtypeStruct((width, depth), BF16), MARK),
        grid=(width // BLK // group,),
        in_specs=[pl.BlockSpec((depth, group * BLK), lambda i: (0, i))] + waits(deps),
        out_specs=(pl.BlockSpec((group * BLK, depth), lambda i: (i, 0)), mark_spec()),
        compiler_params=params(50 * MIB),
        cost_estimate=pl.CostEstimate(
            flops=0, bytes_accessed=4 * depth * width, transcendentals=0
        ),
        name="turned_weight",
    )(weight, *deps)


def transposed(pieces, rows, width, deps):
    step_cols = 1024
    count = len(pieces)

    def kernel(*refs):
        token_refs = refs[:count]
        out, done, held, sems = refs[count + len(deps) :]
        mark(done)
        load_pieces(pieces, token_refs, held, sems)
        step = pl.program_id(0)
        for j in range(step_cols // BLK):
            out[j * BLK : (j + 1) * BLK, :] = held[:, block_at(step * (step_cols // BLK) + j)].T

    return pl.pallas_call(
        kernel,
        out_shape=(jax.ShapeDtypeStruct((width, rows), BF16), MARK),
        grid=(width // step_cols,),
        in_specs=[pl.BlockSpec(memory_space=pl.ANY)] * count + waits(deps),
        out_specs=(pl.BlockSpec((step_cols, rows), lambda i: (i, 0)), mark_spec()),
        scratch_shapes=[
            pltpu.VMEM((rows, width), BF16),
            pltpu.SemaphoreType.DMA((copy_count(pieces),)),
        ],
        compiler_params=params(50 * MIB),
        cost_estimate=pl.CostEstimate(
            flops=0, bytes_accessed=4 * rows * width, transcendentals=0
        ),
        name="transposed",
    )(*[piece[0] for piece in pieces], *deps)


def chip_share(keep, received, s, chunk_rows, deps):
    width = keep.shape[2]

    def kernel(a, b, *refs):
        refs[len(deps)][...] = (a[...].astype(F32) + b[...].astype(F32)).astype(BF16)

    spec = pl.BlockSpec((1, chunk_rows, width), lambda i: (i, s, 0))
    return pl.pallas_call(
        kernel,
        out_shape=jax.ShapeDtypeStruct((2, chunk_rows, width), BF16),
        grid=(2,),
        in_specs=[spec, spec] + waits(deps),
        out_specs=pl.BlockSpec((1, chunk_rows, width), lambda i: (i, 0, 0)),
        compiler_params=params(12 * chunk_rows * width),
        cost_estimate=pl.CostEstimate(
            flops=2 * chunk_rows * width, bytes_accessed=12 * chunk_rows * width, transcendentals=0
        ),
        name="chip_share",
    )(keep, received, *deps)


def cotangents(keep, received, arrived, incoming, chunk, chunk_rows, before, deps):
    width = keep.shape[2]
    cols = column_group(width // BLK) * BLK
    unread = list(before) + list(deps)

    def kernel(a, b, *refs):
        others = refs[: len(arrived)]
        cot_in = refs[len(arrived)]
        hidden, cots, done = refs[len(arrived) + 1 + len(unread) :]
        mark(done)
        sums = []
        for proj in range(2):
            total = a[proj].astype(F32) + b[proj].astype(F32)
            for other in others:
                total = total + other[proj].astype(F32)
            sums.append(total)
        gate_sum, up_sum = sums
        sigmoid_gate = jax.nn.sigmoid(gate_sum)
        silu_gate = gate_sum * sigmoid_gate
        hidden[...] = (silu_gate * up_sum).astype(BF16)
        value = cot_in[...].astype(F32)
        slope = sigmoid_gate * (1.0 + gate_sum * (1.0 - sigmoid_gate))
        cots[0] = (value * up_sum * slope).astype(BF16)
        cots[1] = (value * silu_gate).astype(BF16)

    both = pl.BlockSpec((2, chunk_rows, cols), lambda i: (0, 0, i))
    return pl.pallas_call(
        kernel,
        out_shape=(
            jax.ShapeDtypeStruct(incoming.shape, BF16),
            jax.ShapeDtypeStruct((2, chunk_rows, width), BF16),
            MARK,
        ),
        grid=(width // cols,),
        in_specs=[both] * (2 + len(arrived))
        + [pl.BlockSpec((chunk_rows, cols), lambda i: (chunk, i))]
        + waits(unread),
        out_specs=(pl.BlockSpec((chunk_rows, cols), lambda i: (chunk, i)), both, mark_spec()),
        input_output_aliases={3 + len(arrived) + n: n for n in range(len(before))},
        compiler_params=params(24 * (3 + len(arrived)) * chunk_rows * cols),
        cost_estimate=pl.CostEstimate(
            flops=20 * chunk_rows * width,
            bytes_accessed=20 * chunk_rows * width,
            transcendentals=chunk_rows * width,
        ),
        name="cotangents",
    )(keep, received, *arrived, incoming, *unread)


def reached_pairs(pieces, rows, width, gate_kept, up_kept, same_example, deps):
    keep, blocks = gate_kept.shape
    group = column_group(blocks)
    row_blocks = width // BLK
    count = len(pieces)

    def kernel(gk, uk, *refs):
        token_refs = refs[:count]
        same = refs[count]
        out, done, held, pairs, sems = refs[count + 1 + len(deps) :]
        mark(done)
        load_pieces(pieces, token_refs, held, sems)
        step = pl.program_id(0)

        @pl.when(step == 0)
        def _():
            def some(i, carry):
                for n in range(8):
                    feats = held[:, block_at(i * 8 + n)]
                    pairs[i * 8 + n] = lax.dot_general(
                        feats, feats, (((1,), (1,)), ((), ())), preferred_element_type=F32
                    )
                return carry

            lax.fori_loop(0, row_blocks // 8, some, 0)

        for j in range(group):
            for proj, kept in enumerate((gk, uk)):
                column = step * group + j
                total = pairs[kept[column]]
                for k in range(1, keep):
                    total = total + pairs[kept[k * blocks + column]]
                out[proj, j] = total * same[...]

    return pl.pallas_call(
        kernel,
        out_shape=(jax.ShapeDtypeStruct((2, blocks, rows, rows), F32), MARK),
        grid_spec=pltpu.PrefetchScalarGridSpec(
            num_scalar_prefetch=2,
            grid=(blocks // group,),
            in_specs=[pl.BlockSpec(memory_space=pl.ANY)] * count
            + [pl.BlockSpec((rows, rows), lambda i, *_: (0, 0))]
            + waits(deps),
            out_specs=(
                pl.BlockSpec((2, group, rows, rows), lambda i, *_: (0, i, 0, 0)),
                mark_spec(),
            ),
            scratch_shapes=[
                pltpu.VMEM((rows, width), BF16),
                pltpu.VMEM((row_blocks, rows, rows), F32),
                pltpu.SemaphoreType.DMA((copy_count(pieces),)),
            ],
        ),
        compiler_params=params(50 * MIB),
        cost_estimate=pl.CostEstimate(
            flops=2 * keep * blocks * rows * rows,
            bytes_accessed=40 * blocks * rows * rows,
            transcendentals=0,
        ),
        name="reached_pairs",
    )(
        gate_kept.reshape(-1),
        up_kept.reshape(-1),
        *[piece[0] for piece in pieces],
        same_example,
        *deps,
    )


def example_squares(reached, cots, member, deps):
    blocks, rows = reached.shape[1:3]
    group = column_group(blocks)
    count = len(cots)

    def kernel(*refs):
        cot_refs = refs[:count]
        reach, members = refs[count : count + 2]
        out, total = refs[count + 2 + len(deps) :]
        step = pl.program_id(0)

        @pl.when(step == 0)
        def _():
            total[...] = jnp.zeros_like(total)

        added = total[...]
        for j in range(group):
            cols = slice(j * BLK, (j + 1) * BLK)
            for proj in range(2):
                shaped = jnp.concatenate([ref[proj, :, cols] for ref in cot_refs], axis=0)
                own = lax.dot_general(
                    shaped, shaped, (((1,), (1,)), ((), ())), preferred_element_type=F32
                )
                added = added + own * reach[proj, j]
        total[...] = added

        @pl.when(step == pl.num_programs(0) - 1)
        def _():
            per_token = jnp.sum(total[...], axis=1, keepdims=True)
            per_example = jnp.sum(per_token * members[...], axis=0, keepdims=True)
            out[...] = jnp.broadcast_to(per_example, out.shape)

    cot_rows = cots[0].shape[1]
    return pl.pallas_call(
        kernel,
        out_shape=jax.ShapeDtypeStruct((8, LANES), F32),
        grid=(blocks // group,),
        in_specs=[pl.BlockSpec((2, cot_rows, group * BLK), lambda i: (0, 0, i))] * count
        + [
            pl.BlockSpec((2, group, rows, rows), lambda i: (0, i, 0, 0)),
            pl.BlockSpec((rows, LANES), lambda i: (0, 0)),
        ]
        + waits(deps),
        out_specs=pl.BlockSpec((8, LANES), lambda i: (0, 0)),
        scratch_shapes=[pltpu.VMEM((rows, rows), F32)],
        compiler_params=params((16 * group + 8) * rows * rows + 8 * rows * group * BLK),
        cost_estimate=pl.CostEstimate(
            flops=8 * blocks * rows * rows * BLK,
            bytes_accessed=8 * blocks * rows * rows,
            transcendentals=0,
        ),
        name="example_squares",
    )(*cots, reached, member, *deps)


def token_backward(cots, width, gate_own, up_own, gate_turned, up_turned, deps):
    slots, blocks = gate_own.shape
    group = column_group(blocks)
    depth = slots * BLK
    count = len(cots)
    piece_rows = cots[0].shape[1]
    rows = piece_rows * count
    half = rows // CORES

    def kernel(gk, uk, *refs):
        cot_refs = refs[:count]
        wg, wu = refs[count : count + 2]
        keep, send, done, total = refs[count + 2 + len(deps) :]
        mark(done)
        step = pl.program_id(0)

        @pl.when(step == 0)
        def _():
            total[...] = jnp.zeros_like(total)

        for j in range(group):
            cols = slice(j * BLK, (j + 1) * BLK)
            for proj, (kept, weight) in enumerate(((gk, wg), (uk, wu))):
                cot = jnp.concatenate([ref[proj, :, cols] for ref in cot_refs], axis=0)
                back = jnp.dot(cot, weight[cols, :], preferred_element_type=F32)
                for k in range(slots):
                    place = kept[k * blocks + step * group + j]
                    total[place] = total[place] + back[:, k * BLK : (k + 1) * BLK]

        @pl.when(step == pl.num_programs(0) - 1)
        def _():
            for i in range(width // BLK):
                cols = slice(i * BLK, (i + 1) * BLK)
                keep[:, cols] = total[i, :half].astype(BF16)
                send[:, cols] = total[i, half:].astype(BF16)

    weight_spec = pl.BlockSpec((group * BLK, depth), lambda i, *_: (i, 0))
    out = jax.ShapeDtypeStruct((half, width), BF16)
    out_spec = pl.BlockSpec((half, width), lambda i, *_: (0, 0))
    return pl.pallas_call(
        kernel,
        out_shape=(out, out, MARK),
        grid_spec=pltpu.PrefetchScalarGridSpec(
            num_scalar_prefetch=2,
            grid=(blocks // group,),
            in_specs=[
                pl.BlockSpec((2, piece_rows, group * BLK), lambda i, *_: (0, 0, i))
            ]
            * count
            + [weight_spec] * 2
            + waits(deps),
            out_specs=(out_spec, out_spec, mark_spec()),
            scratch_shapes=[pltpu.VMEM((width // BLK, rows, BLK), F32)],
        ),
        compiler_params=params(50 * MIB),
        cost_estimate=pl.CostEstimate(
            flops=8 * rows * depth * blocks * BLK,
            bytes_accessed=4 * depth * blocks * BLK + 2 * rows * width,
            transcendentals=0,
        ),
        name="token_backward",
    )(gate_own.reshape(-1), up_own.reshape(-1), *cots, gate_turned, up_turned, *deps)


def added_cuts(arrays, outputs, deps):
    count = len(arrays)

    def kernel(*refs):
        *outs, done = refs[count + len(deps) :]
        mark(done)
        for cuts, out in zip(outputs, outs, strict=True):
            target = 0
            for which, row, rows, col, cols in cuts:
                at = (slice(row, row + rows), slice(col, col + cols))
                total = refs[which[0]][at].astype(F32)
                for n in which[1:]:
                    total = total + refs[n][at].astype(F32)
                out[target : target + rows, :] = total.astype(BF16)
                target += rows

    size = sum(array.shape[0] * array.shape[1] for array in arrays)
    return pl.pallas_call(
        kernel,
        out_shape=[
            jax.ShapeDtypeStruct((sum(cut[2] for cut in cuts), cuts[0][4]), BF16)
            for cuts in outputs
        ]
        + [MARK],
        in_specs=[pl.BlockSpec(memory_space=pltpu.VMEM)] * count + waits(deps),
        out_specs=[pl.BlockSpec(memory_space=pltpu.VMEM)] * (len(outputs) + 1),
        compiler_params=params(4 * MIB),
        cost_estimate=pl.CostEstimate(flops=size, bytes_accessed=4 * size, transcendentals=0),
        name="added_cuts",
    )(*arrays, *deps)


def weight_gradients(turned, cots, factors, gate_own, up_own, deps):
    slots, blocks = gate_own.shape
    group = column_group(blocks)
    depth = slots * BLK
    chunks = len(turned)
    per_chunk = len(cots) // chunks
    piece_rows = cots[0].shape[1]
    rows = piece_rows * per_chunk
    width = turned[0].shape[0]
    steps = blocks // group

    def kernel(gk, uk, *refs):
        token_refs = refs[:chunks]
        cot_refs = refs[chunks : chunks + len(cots)]
        factor = refs[chunks + len(cots)]
        gate_out, up_out, done = refs[chunks + len(cots) + 1 + len(deps) :]
        mark(done)
        step = pl.program_id(0)
        for j in range(group):
            cols = slice(j * BLK, (j + 1) * BLK)
            for proj, (kept, out) in enumerate(((gk, gate_out), (uk, up_out))):
                total = None
                for chunk in range(chunks):
                    cot = jnp.concatenate(
                        [
                            ref[proj, :, cols]
                            for ref in cot_refs[chunk * per_chunk : (chunk + 1) * per_chunk]
                        ],
                        axis=0,
                    )
                    scaled = (
                        factor[chunk * rows : (chunk + 1) * rows, :] * cot.astype(F32)
                    ).astype(BF16)
                    feats = [
                        token_refs[chunk][block_at(kept[k * blocks + step * group + j]), :]
                        for k in range(slots)
                    ]
                    term = jnp.dot(
                        jnp.concatenate(feats, axis=0), scaled, preferred_element_type=F32
                    )
                    total = term if total is None else total + term
                out[:, cols] = total.astype(BF16)

    out = jax.ShapeDtypeStruct((depth, blocks * BLK), BF16)
    out_spec = pl.BlockSpec((depth, group * BLK), lambda i, *_: (0, i))
    operands = [gate_own.reshape(-1), up_own.reshape(-1), *turned, *cots, factors]
    return pl.pallas_call(
        kernel,
        out_shape=(out, out, MARK),
        grid_spec=pltpu.PrefetchScalarGridSpec(
            num_scalar_prefetch=2,
            grid=(steps,),
            in_specs=[
                pl.BlockSpec((width, rows), lambda i, *_: (0, 0), pipeline_mode=pl.Buffered(1))
            ]
            * chunks
            + [pl.BlockSpec((2, piece_rows, group * BLK), lambda i, *_: (0, 0, i))]
            * len(cots)
            + [pl.BlockSpec((rows * chunks, LANES), lambda i, *_: (0, 0))]
            + waits(deps),
            out_specs=(out_spec, out_spec, mark_spec()),
        ),
        compiler_params=params(55 * MIB),
        cost_estimate=pl.CostEstimate(
            flops=8 * rows * chunks * depth * steps * group * BLK,
            bytes_accessed=4 * depth * steps * group * BLK + 2 * rows * chunks * width,
            transcendentals=0,
        ),
        name="weight_gradients",
    )(*operands, *deps)


def shards(
    tokens,
    hidden_cotangent,
    gate_weight,
    up_weight,
    gate_kept,
    up_kept,
    example_number,
    clip_norm,
    fsdp,
    tensor,
):
    chips = fsdp // CORES
    own_rows, own_features = tokens.shape
    blocks = gate_kept.shape[1]
    width = own_features * tensor
    blocks_each = own_features // BLK
    chunk_rows = own_rows // CHUNKS
    first_rows = chunk_rows // 2
    half = chips * chunk_rows
    rows = CORES * half
    z = lax.axis_index("tensor")
    f = lax.axis_index("fsdp")

    def from_chip(value, back):
        pairs = [
            (i, ((i // CORES + back) % chips) * CORES + i % CORES) for i in range(fsdp)
        ]
        return lax.ppermute(value, "fsdp", pairs)

    def from_core(value):
        return lax.ppermute(value, "fsdp", [(i, i ^ 1) for i in range(fsdp)])

    def from_rank(value, core, back):
        pairs = [
            (i, ((i // CORES + back) % chips) * CORES + (i % CORES + core) % CORES)
            for i in range(fsdp)
        ]
        return lax.ppermute(value, "fsdp", pairs)

    def from_tensor(value, back):
        return lax.ppermute(value, "tensor", [(i, (i + back) % tensor) for i in range(tensor)])

    def renumber(kept):
        return jnp.mod(z - kept // blocks_each, tensor) * blocks_each + kept % blocks_each

    gate_all, up_all = renumber(gate_kept), renumber(up_kept)
    slots = gate_weight.shape[0] // BLK
    gate_own = lax.dynamic_slice_in_dim(gate_all, f * slots, slots, 0)
    up_own = lax.dynamic_slice_in_dim(up_all, f * slots, slots, 0)

    lanes = jnp.arange(LANES, dtype=jnp.int32)
    member = (example_number[:, None] == lanes[None, :]).astype(F32)
    same_example = (example_number[:, None] == example_number[None, :]).astype(F32)

    def piece(array, core, s, p):
        target = core * half + s * chunk_rows
        return (array, [(0, array.shape[0], target)], p * own_features)

    part_0, part_1 = rows_of(tokens, [(0, chunk_rows), (chunk_rows, chunk_rows)], ())
    along = [part_0] + [from_tensor(part_0, p) for p in range(1, tensor)]
    stack = jnp.concatenate([part_1] + [from_chip(part_1, s) for s in range(1, chips)], axis=0)
    moved = {0: [from_chip(part_0, s) for s in range(1, chips)]}
    last = 0
    for p in sorted(range(1, tensor), key=lambda p: min(p, tensor - p)):
        along[p], stack, *moved[last] = after([along[p], stack] + moved[last], ())
        moved[p] = [from_chip(along[p], s) for s in range(1, chips)]
        last = p
    pieces_0, mine = [], []
    for p in range(tensor):
        mine.append((along[p], [(0, chunk_rows, 0)], p * own_features))
        for s, array in enumerate([along[p]] + moved[p]):
            pieces_0 += [piece(array, 0, s, p), piece(from_core(array), 1, s, p)]
    middle = tensor // 2
    ring = [stack]

    def step_on():
        return [from_tensor(ring[-1], 1)] if len(ring) < tensor else []

    def arrive(moving, arrays, deps):
        if moving + arrays:
            moving = after(moving + arrays, deps)
            ring.extend(moving[: len(moving) - len(arrays)])
        return moving[len(moving) - len(arrays) :]

    moving = step_on()
    keep_0, send_0 = forward(
        pieces_0, rows, width, gate_own, up_own, gate_weight, up_weight, [stack]
    )
    (send_0,) = arrive(moving, [send_0], ())
    moving = step_on()
    received_0 = from_core(send_0)
    gate_turned, gate_done = turned_weight(gate_weight, [send_0])
    arrive(moving, [], [gate_done])
    moving = step_on()
    leaving_0 = [
        chip_share(keep_0, received_0, s, chunk_rows, [gate_done]) for s in range(1, chips)
    ]
    up_turned, up_done = turned_weight(up_weight, leaving_0)
    arrive(moving, [], [up_done])
    while len(ring) < tensor:
        ring += step_on()
    tokens_0, tokens_0_done = transposed(pieces_0, rows, width, [up_done, ring[-1]])
    arrived_0 = [from_chip(part, -s - 1) for s, part in enumerate(leaving_0)]
    pieces_1 = []
    for p, array in enumerate(ring):
        mine.append((array, [(0, chunk_rows, chunk_rows)], p * own_features))
        pieces_1 += [piece(array, 0, 0, p), piece(from_core(array), 1, 0, p)]

    hidden_0, cots_0, cots_0_done = cotangents(
        keep_0, received_0, arrived_0, hidden_cotangent, 0, chunk_rows, (), [tokens_0_done]
    )
    far_0 = [from_chip(cots_0, s) for s in range(1, chips)]
    keep_1, send_1 = forward(
        pieces_1, rows, width, gate_own, up_own, gate_weight, up_weight, [cots_0_done]
    )
    *far_0, send_1 = after(far_0 + [send_1], [keep_1])
    received_1 = from_core(send_1)
    leaving_1 = [chip_share(keep_1, received_1, s, chunk_rows, ()) for s in range(1, chips)]
    arrived_1 = [from_chip(part, -s - 1) for s, part in enumerate(leaving_1)]
    every_0 = [cots_0] + far_0 + [from_core(part) for part in [cots_0] + far_0]
    back_0 = token_backward(
        every_0, width, gate_own, up_own, gate_turned, up_turned, leaving_1
    )
    *arrived_1, sent = after(arrived_1 + [back_0[1]], ())
    received = from_core(sent)
    hidden, cots_1, cots_1_done = cotangents(
        keep_1, received_1, arrived_1, hidden_cotangent, 1, chunk_rows, [hidden_0], [back_0[2]]
    )
    far_1 = [from_chip(cots_1, s) for s in range(1, chips)]

    def leave(keep, received, count, deps):
        rest = chunk_rows - count
        outputs = [
            [
                ((0, 1), s * chunk_rows, count, p * own_features, own_features)
                for s in range(chips)
            ]
            for p in range(tensor)
        ]
        if rest:
            outputs += [[((0, 1), s * chunk_rows + count, rest, 0, width)] for s in range(chips)]
        outs = added_cuts([keep, received], outputs, deps)
        return outs[:tensor], outs[tensor:-1], outs[-1]

    def over_tensor_first(stacks):
        return [stacks[0]] + [from_tensor(stacks[p], -p) for p in range(1, tensor)]

    def then_chips(stacks, count, deps):
        every = tuple(range(len(stacks)))
        outputs = [[(every, s * count, count, 0, own_features)] for s in range(chips)]
        outs = added_cuts(stacks, outputs, deps)
        return [outs[0]] + [from_chip(outs[s], -s) for s in range(1, chips)], outs[-1]

    parts_0, _, parts_0_done = leave(back_0[0], received, chunk_rows, [cots_1_done])
    crossing_0 = over_tensor_first(parts_0)
    reached, _ = reached_pairs(
        mine, own_rows, width, gate_all, up_all, same_example, [parts_0_done]
    )
    early = [p for p in range(1, tensor) if p != middle]
    partial = example_squares(reached, [cots_0, cots_1], member, ())
    apart = [from_tensor(partial, p) for p in range(1, tensor)]
    ordered = after(far_1 + [crossing_0[p] for p in early] + apart, [partial])
    far_1 = list(ordered[: len(far_1)])
    apart = list(ordered[len(far_1) + len(early) :])
    for p, array in zip(early, ordered[len(far_1) : len(far_1) + len(early)], strict=True):
        crossing_0[p] = array
    every_1 = [cots_1] + far_1 + [from_core(part) for part in [cots_1] + far_1]
    tokens_1, tokens_1_done = transposed(pieces_1, rows, width, ordered[:1])
    back_1 = token_backward(
        every_1, width, gate_own, up_own, gate_turned, up_turned, [tokens_1_done]
    )
    crossing_0[middle], sent, *apart = after([crossing_0[middle], back_1[1]] + apart, ())
    squares = partial[0]
    for array in apart:
        squares = squares + array[0]
    threshold = clip_norm[0] * math.sqrt(D * FFW)
    factor = threshold / jnp.maximum(jnp.sqrt(squares), threshold)
    own_factor = jnp.sum(member * factor[None, :], axis=1)
    factors_near = [own_factor] + [
        from_rank(own_factor, core, s) for core in range(CORES) for s in range(chips) if core or s
    ]
    received = from_core(sent)
    final_0, final_0_done = then_chips(crossing_0, chunk_rows, [back_1[2]])
    factors = jnp.concatenate(
        [
            part[chunk * chunk_rows : (chunk + 1) * chunk_rows]
            for chunk in range(CHUNKS)
            for part in factors_near
        ]
    )
    factors = jnp.broadcast_to(factors[:, None], (rows * CHUNKS, LANES))

    parts_1, rest_1, parts_1_done = leave(back_1[0], received, first_rows, [final_0_done])
    crossing_1 = over_tensor_first(parts_1)
    over_chips = [rest_1[0]] + [from_chip(rest_1[s], -s) for s in range(1, chips)]
    rest = chunk_rows - first_rows

    gate_grad, up_grad, grads_done = weight_gradients(
        [tokens_0, tokens_1], every_0 + every_1, factors, gate_own, up_own, [parts_1_done]
    )
    every = tuple(range(chips))
    shares = added_cuts(
        over_chips,
        [[(every, 0, rest, p * own_features, own_features)] for p in range(tensor)],
        [grads_done],
    )
    late = [shares[0]] + [from_tensor(shares[p], -p) for p in range(1, tensor)]
    final_1, _ = then_chips(crossing_1, first_rows, [grads_done])
    parts, cuts = [], []
    for arrays, count in ((final_0, chunk_rows), (final_1, first_rows), (late, rest)):
        places = tuple(range(len(parts), len(parts) + len(arrays)))
        parts += arrays
        cuts.append((places, 0, count, 0, own_features))
    token_grad, _ = added_cuts(parts, [cuts], [grads_done])
    return (hidden, gate_grad, up_grad, token_grad)


def solution(mesh):
    rows_by_columns = P(("groups", "fsdp"), "tensor")
    return jax.shard_map(
        functools.partial(shards, fsdp=mesh.shape["fsdp"], tensor=mesh.shape["tensor"]),
        mesh=mesh,
        in_specs=(
            rows_by_columns,
            rows_by_columns,
            P("fsdp", "tensor"),
            P("fsdp", "tensor"),
            P(None, "tensor"),
            P(None, "tensor"),
            P(("groups", "fsdp")),
            P(),
        ),
        out_specs=(rows_by_columns,) * 4,
        check_vma=False,
    )
```
